128 devices in a mesh: grp: 4 (over z_lo, core), dev: 32 (over z_hi, x, y).
Axes of the slice: x: 4, y: 4, z: 4 (z_hi: 2, z_lo: 2; z = z_hi * 2 + z_lo), core: 2. Of those that a mesh axis runs over, the one named last changes fastest.
Arguments:
- pressure_old: float32 [128, 256, 256], P(('grp', 'dev')), may hold values from -6 to 6
- strain_change: float32 [128, 256, 256], P(('grp', 'dev')), may hold values from -3 to 3
- storage: float32 [128, 256, 256], P(('grp', 'dev')), may hold values from 0.05 to 0.5
- trans_x: float32 [128, 256, 256], P(('grp', 'dev')), may hold values from 0.3 to 3
- trans_y: float32 [128, 256, 256], P(('grp', 'dev')), may hold values from 0.3 to 3
- trans_z: float32 [128, 256, 256], P(('grp', 'dev')), may hold values from 0.3 to 3
- displacement_old: float32 [3, 128, 256, 256], P(None, 'grp', 'dev'), may hold values from -6 to 6
- modulus: float32 [128, 256, 256], P('grp', 'dev'), may hold values from 0.01 to 0.05
- perf_cell: int32 [512, 128], P(('grp', 'dev')), may hold values from 0 to 65535
- perf_well: int32 [512], P(('grp', 'dev')), may hold values from 0 to 255, as said below
- perf_count: int32 [512], P(('grp', 'dev')), may hold values from 1 to 128, as said below
- perf_index: float32 [512, 128], P(('grp', 'dev')), may hold values from 0.5 to 5
- well_rate: float32 [256], replicated, may hold values from -600 to 600
Outputs:
- pressure: float32 [128, 256, 256], P(('grp', 'dev'))
- displacement: float32 [3, 128, 256, 256], P(None, 'grp', 'dev')
- strain: float32 [128, 256, 256], P(('grp', 'dev'))
The draws below stay inside these ranges and needn't reach their ends.
Inputs may be any that keep to these rules, and one draw needn't show every extreme that they name: `perf_well`: every well owns exactly two perforation blocks, which lie on devices drawn from the seed. `perf_count`: every draw has a block with all 128 rows live and a block with one live row.
All inputs are finite; a program needn't handle non-finite values.
Results may differ from the reference program's by a relative error of at most 0.0001.
Values sent between devices are 32-bit elements; how exact they have to be, the bound alone decides.
A program may use at most 64 MiB of HBM per device.

```python
import math
import jax
import jax.numpy as jnp

CZ = 256
BLOCKS = 4
ROWS = 128
FLOW_SWEEPS = 4
MECH_SWEEPS = 6
NX = 128
NY = 256
CELLS = 65536
NBLK = 512
WELLS = 256


def draw_perf_well(key, part):
    key = jax.random.fold_in(key, 11)
    shuffled = jax.random.permutation(key, NBLK)
    return (shuffled % WELLS).astype(jnp.int32)


def draw_perf_count(key, part):
    key = jax.random.fold_in(key, 23)
    key_count, key_full, key_single = jax.random.split(key, 3)
    counts = jax.random.randint(key_count, (NBLK,), 1, ROWS + 1, dtype=jnp.int32)
    full_block = jax.random.randint(key_full, (), 0, NBLK, dtype=jnp.int32)
    offset = jax.random.randint(key_single, (), 1, NBLK, dtype=jnp.int32)
    counts = counts.at[full_block].set(ROWS)
    counts = counts.at[(full_block + offset) % NBLK].set(1)
    return counts.astype(jnp.int32)


def set_ends(array, stream_key, least, top_value):
    extent = array.shape
    index_at = [jax.random.randint(jax.random.fold_in(stream_key, axis), (), 0, extent[axis]) for axis in range(len(extent))]
    array = array.at[tuple(index_at)].set(least)
    longest = extent.index(max(extent))
    index_at[longest] = (index_at[longest] + 1) % extent[longest]
    return array.at[tuple(index_at)].set(top_value)


def block_scale(rng, dims, cuts, least, largest):
    def one(dim, parts):
        heights = jax.random.uniform(jax.random.fold_in(jax.random.fold_in(rng, 6), dim), (parts,), jnp.float32, least / len(cuts), largest / len(cuts))
        return jnp.repeat(jnp.exp(heights), dims[dim] // parts).reshape((-1,) + (1,) * (len(dims) - dim - 1))

    gain = one(*cuts[0])
    for cut in cuts[1:]:
        gain = gain * one(*cut)
    return gain


def noise(stream_key, extent, scale, bound, pieces=(), kind=jnp.bfloat16):
    level = block_scale(stream_key, extent, pieces, -0.22, 0.18) if pieces else 1.0
    entries = jax.random.normal(stream_key, extent, jnp.float32) * scale * level
    return jnp.minimum(jnp.maximum(entries, -bound), bound).astype(kind)


def setup_inputs(seed: int = 0) -> dict:
    streams_of = jax.random.split(jax.random.key(seed), 14)
    pressure_old = noise(streams_of[0], (NX, NY, CZ), 1.0, 6.0, ((0, 128),), jnp.float32)
    strain_change = noise(streams_of[1], (NX, NY, CZ), 0.5, 3.0, ((0, 128),), jnp.float32)
    storage = jnp.clip(jnp.exp(math.log(0.5) - 2.3025851 * jax.random.uniform(streams_of[2], (NX, NY, CZ), jnp.float32) ** block_scale(streams_of[2], (NX, NY, CZ), ((0, 128),), -0.2, 0.2)), 0.05, 0.5)
    trans_x = jnp.clip(jnp.exp(math.log(3.0) - 2.3025851 * jax.random.uniform(streams_of[3], (NX, NY, CZ), jnp.float32) ** block_scale(streams_of[3], (NX, NY, CZ), ((0, 128),), -0.2, 0.2)), 0.3, 3.0)
    trans_y = jnp.clip(jnp.exp(math.log(3.0) - 2.3025851 * jax.random.uniform(streams_of[4], (NX, NY, CZ), jnp.float32) ** block_scale(streams_of[4], (NX, NY, CZ), ((0, 128),), -0.2, 0.2)), 0.3, 3.0)
    trans_z = jnp.clip(jnp.exp(math.log(3.0) - 2.3025851 * jax.random.uniform(streams_of[5], (NX, NY, CZ), jnp.float32) ** block_scale(streams_of[5], (NX, NY, CZ), ((0, 128),), -0.2, 0.2)), 0.3, 3.0)
    displacement_old = noise(streams_of[6], (3, NX, NY, CZ), 1.0, 6.0, ((1, 4), (2, 32)), jnp.float32)
    modulus = jnp.clip(jnp.exp(math.log(0.05) - 1.609438 * jax.random.uniform(streams_of[7], (NX, NY, CZ), jnp.float32) ** block_scale(streams_of[7], (NX, NY, CZ), ((0, 4), (1, 32)), -0.2, 0.2)), 0.01, 0.05)
    perf_cell = set_ends(jax.random.randint(streams_of[8], (NBLK, ROWS), 0, CELLS), jax.random.fold_in(streams_of[8], 1), 0, CELLS - 1).astype(jnp.int32)
    perf_well = draw_perf_well(jax.random.fold_in(streams_of[13], 71), 0)
    perf_count = draw_perf_count(jax.random.fold_in(streams_of[13], 71), 0)
    perf_index = jnp.clip(jnp.exp(math.log(5.0) - 2.3025851 * jax.random.uniform(streams_of[11], (NBLK, ROWS), jnp.float32) ** block_scale(streams_of[11], (NBLK, ROWS), ((0, 128),), -0.2, 0.2)), 0.5, 5.0)
    well_rate = noise(streams_of[12], (WELLS,), 100.0, 600.0, (), jnp.float32)
    return {"pressure_old": pressure_old, "strain_change": strain_change, "storage": storage, "trans_x": trans_x, "trans_y": trans_y, "trans_z": trans_z, "displacement_old": displacement_old, "modulus": modulus, "perf_cell": perf_cell, "perf_well": perf_well, "perf_count": perf_count, "perf_index": perf_index, "well_rate": well_rate}


biot_coeff = 0.8
relax_factor = 0.6
coupling_ratio = 1.5


def above_z(values):
    return jnp.concatenate([values[..., 1:], jnp.zeros_like(values[..., :1])], axis=-1)


def below_z(values):
    return jnp.concatenate([jnp.zeros_like(values[..., :1]), values[..., :-1]], axis=-1)


def gradients(field):
    grad_x = field[0, 2:, :] - field[0, :-2, :]
    grad_y = field[1, :, 2:] - field[1, :, :-2]
    grad_z = above_z(field[2]) - below_z(field[2])
    return grad_x, grad_y, grad_z


def stiffness(field):
    column_sum = field + above_z(field) + below_z(field)
    row_sum = column_sum[:, :, :-2] + column_sum[:, :, 1:-1] + column_sum[:, :, 2:]
    box_sum = row_sum[:, :-2] + row_sum[:, 1:-1] + row_sum[:, 2:]
    grad_x, grad_y, grad_z = gradients(field)
    along_x = grad_y + grad_z[:, 1:-1]
    along_y = grad_x + grad_z[1:-1]
    along_z = grad_x[:, 1:-1] + grad_y[1:-1]
    mixed_terms = jnp.stack([along_x[2:] - along_x[:-2], along_y[:, 2:] - along_y[:, :-2], above_z(along_z) - below_z(along_z)])
    return 27.0 * field[:, 1:-1, 1:-1] - box_sum - (0.25 * coupling_ratio) * mixed_terms


def divergence(field):
    grad_x, grad_y, grad_z = gradients(field)
    return 0.5 * (grad_x[:, 1:-1] + grad_y[1:-1] + grad_z[1:-1, 1:-1])


def forces(press):
    force_x = press[2:, 1:-1] - press[:-2, 1:-1]
    force_y = press[1:-1, 2:] - press[1:-1, :-2]
    middle = press[1:-1, 1:-1]
    force_z = above_z(middle) - below_z(middle)
    return (-0.5 * biot_coeff) * jnp.stack([force_x, force_y, force_z])


def pad_plane(field):
    return jnp.pad(field, ((0, 0), (1, 1), (1, 1), (0, 0)))


def reference(pressure_old, strain_change, storage, trans_x, trans_y, trans_z, displacement_old, modulus, perf_cell, perf_well, perf_count, perf_index, well_rate):
    block_count = perf_cell.shape[0]
    total_cells = NX * NY * CZ
    owner_offset = (jnp.arange(block_count, dtype=jnp.int32) // BLOCKS) * CELLS
    flat_cell = (perf_cell + owner_offset[:, None]).reshape(-1).astype(jnp.int32)
    live_rows = (jnp.arange(ROWS, dtype=jnp.int32)[None, :] < perf_count[:, None]).astype(jnp.float32)
    weight = perf_index * live_rows
    member = (perf_well[:, None] == jnp.arange(WELLS, dtype=jnp.int32)[None, :]).astype(jnp.float32)
    strength = jnp.sum(member * jnp.sum(weight, axis=1)[:, None], axis=0)
    well_cells = jnp.zeros((total_cells,), jnp.float32).at[flat_cell].add(weight.reshape(-1)).reshape(pressure_old.shape)
    east_face = trans_x.at[-1].set(0.0)
    west_face = jnp.concatenate([jnp.zeros_like(trans_x[:1]), trans_x[:-1]], axis=0)
    north_face = trans_y.at[:, -1].set(0.0)
    south_face = jnp.concatenate([jnp.zeros_like(trans_y[:, :1]), trans_y[:, :-1]], axis=1)
    upper_face = trans_z.at[:, :, -1].set(0.0)
    lower_face = jnp.concatenate([jnp.zeros_like(trans_z[:, :, :1]), trans_z[:, :, :-1]], axis=2)
    diagonal_sum = storage + east_face + west_face + north_face + south_face + upper_face + lower_face + well_cells
    base_term = storage * pressure_old - biot_coeff * strain_change
    pressure = pressure_old
    for sweep_index in range(FLOW_SWEEPS):
        padded = jnp.pad(pressure, 1)
        beside = east_face * padded[2:, 1:-1, 1:-1] + west_face * padded[:-2, 1:-1, 1:-1]
        beside = beside + north_face * padded[1:-1, 2:, 1:-1] + south_face * padded[1:-1, :-2, 1:-1]
        beside = beside + upper_face * padded[1:-1, 1:-1, 2:] + lower_face * padded[1:-1, 1:-1, :-2]
        sampled = pressure.reshape(-1)[flat_cell].reshape(block_count, ROWS)
        block_sum = jnp.sum(weight * sampled, axis=1)
        well_sum = jnp.sum(member * block_sum[:, None], axis=0)
        bottom = (well_rate + well_sum) / strength
        block_bottom = jnp.sum(member * bottom[None, :], axis=1)
        inflow = jnp.zeros((total_cells,), jnp.float32).at[flat_cell].add((weight * block_bottom[:, None]).reshape(-1)).reshape(pressure.shape)
        pressure = (base_term + beside + inflow) / diagonal_sum
    force_field = forces(jnp.pad(pressure, ((1, 1), (1, 1), (0, 0))))
    inverse = 1.0 / (26.0 * modulus)
    displacement = displacement_old
    for sweep_index in range(MECH_SWEEPS):
        displacement = displacement + relax_factor * (force_field - modulus * stiffness(pad_plane(displacement))) * inverse
    strain = divergence(pad_plane(displacement))
    return pressure, displacement, strain
```

```python
import functools

import jax
import jax.numpy as jnp
from jax import lax
from jax.experimental import pallas as pl
from jax.experimental.pallas import tpu as pltpu
from jax.sharding import PartitionSpec as P

MESH = pl.DeviceIdType.MESH
F32 = jnp.float32

FLOW_SWEEPS = 4
MECH_SWEEPS = 6
BIOT = 0.8
RELAX = 0.6
COUPLE = 0.375

NG, ND = 4, 32
NF = NG * ND
NY, NZ = 256, 256
XS, YS = 32, 8
HALO = MECH_SWEEPS + 1
XW = XS + 2 * HALO
YW = 3 * YS
BLOCKS = 4

ALPHA = 1.0 - RELAX * 27.0 / 26.0
BETA = RELAX / 26.0


def iota(shape, dim):
    return lax.broadcasted_iota(jnp.int32, shape, dim)


def next_z(v):
    n = v.shape[-1]
    return jnp.where(iota(v.shape, 1) == n - 1, 0.0, pltpu.roll(v, n - 1, 1))


def prev_z(v):
    return jnp.where(iota(v.shape, 1) == 0, 0.0, pltpu.roll(v, 1, 1))


def next_y(v):
    return pltpu.roll(v, v.shape[0] - 1, 0)


def prev_y(v):
    return pltpu.roll(v, 1, 0)


def total(v):
    return jnp.sum(jnp.sum(v, axis=0, keepdims=True), axis=1, keepdims=True)


def kernel(
    p0_h, sc_h, st_h, tx_h, ty_h, tz_h, u_h, mod_h, cell_ref, well_ref, cnt_ref, idx_ref, rate_ref,
    p_out, u_out, s_out,
    press, base, east, west, north, south, upper, lower, rdiag, wells, halo_lo, halo_hi,
    msg0, msg, ag0, ag, masks,
    ppad, pwin, ua, ub, mod, gain, force, tzb, dzb, strain,
    load_sem, uload_sem, halo_send, halo_recv, tx_send, tx_recv, ag_send, ag_recv,
    usend, urecv, xsend, xrecv, pw_send, pw_recv, pw_self, st_send, st_recv, st_self, out_sem,
):
    g = lax.axis_index("grp")
    d = lax.axis_index("dev")
    f = g * ND + d
    first, last = f == 0, f == NF - 1

    def flow_dev(k):
        return (k // ND, lax.rem(k, ND))

    after, before = flow_dev(lax.rem(f + 1, NF)), flow_dev(lax.rem(f + NF - 1, NF))

    plane_loads = [
        pltpu.make_async_copy(src.at[0], dst, load_sem.at[i])
        for i, (src, dst) in enumerate(
            [
                (p0_h, press.at[0]),
                (sc_h, base),
                (st_h, rdiag),
                (tx_h, east),
                (ty_h, north),
                (tz_h, upper),
            ]
        )
    ]
    for c in plane_loads:
        c.start()
    own_u = pltpu.make_async_copy(
        u_h, ua.at[:, pl.ds(HALO, XS), pl.ds(YS, YS)], uload_sem.at[0]
    )
    own_m = pltpu.make_async_copy(
        mod_h, mod.at[pl.ds(HALO, XS), pl.ds(YS, YS)], uload_sem.at[1]
    )
    own_u.start()
    own_m.start()

    barrier = pltpu.get_barrier_semaphore()

    def greet(i, carry):
        pl.semaphore_signal(
            barrier, inc=1, device_id=flow_dev(lax.rem(f + i, NF)), device_id_type=MESH
        )
        return carry

    lax.fori_loop(1, NF, greet, 0)

    @pl.when(d == 0)
    def _():
        ua[:, HALO : HALO + XS, 0:YS, :] = jnp.zeros((3, XS, YS, NZ), F32)
        mod[HALO : HALO + XS, 0:YS, :] = jnp.ones((XS, YS, NZ), F32)

    @pl.when(d == ND - 1)
    def _():
        ua[:, HALO : HALO + XS, 2 * YS :, :] = jnp.zeros((3, XS, YS, NZ), F32)
        mod[HALO : HALO + XS, 2 * YS :, :] = jnp.ones((XS, YS, NZ), F32)

    @pl.when(g == 0)
    def _():
        ua[:, 0:HALO] = jnp.zeros((3, HALO, YW, NZ), F32)
        mod[0:HALO] = jnp.ones((HALO, YW, NZ), F32)
        pwin[0:HALO] = jnp.zeros((HALO, YW, NZ), F32)

    @pl.when(g == NG - 1)
    def _():
        ua[:, HALO + XS :] = jnp.zeros((3, HALO, YW, NZ), F32)
        mod[HALO + XS :] = jnp.ones((HALO, YW, NZ), F32)
        pwin[HALO + XS :] = jnp.zeros((HALO, YW, NZ), F32)

    @pl.when(first)
    def _():
        halo_lo[...] = jnp.zeros(halo_lo.shape, F32)
        west[...] = jnp.zeros((NY, NZ), F32)

    @pl.when(last)
    def _():
        halo_hi[...] = jnp.zeros(halo_hi.shape, F32)

    ppad[0:YS, :] = jnp.zeros((YS, NZ), F32)
    ppad[NY + YS :, :] = jnp.zeros((YS, NZ), F32)

    lane = iota((1, 128), 1)
    weight_sums = []
    for b in range(BLOCKS):
        live = lane < cnt_ref[b : b + 1, :]
        weight = jnp.where(live, idx_ref[b : b + 1, :], 0.0)
        cell = cell_ref[b : b + 1, :]
        row, col = cell // NZ, lax.rem(cell, NZ)
        at_row = iota((NY, 128), 0) == row
        at_col = jnp.where(iota((NZ, 128), 0) == col, 1.0, 0.0).astype(jnp.bfloat16)
        rest = weight
        plane = jnp.zeros((NY, NZ), F32)
        for _ in range(3):
            part = rest.astype(jnp.bfloat16)
            rest = rest - part.astype(F32)
            spread = jnp.where(at_row, part.astype(F32), 0.0).astype(jnp.bfloat16)
            plane = plane + lax.dot_general(
                spread, at_col, (((1,), (1,)), ((), ())), preferred_element_type=F32
            )
        wells[b] = plane
        weight_sums.append(jnp.sum(weight, axis=1, keepdims=True))

    pl.semaphore_wait(barrier, NF - 1)

    for c in plane_loads:
        c.wait()

    def halo_copies(k):
        up = pltpu.make_async_remote_copy(
            press.at[k], halo_lo.at[k], halo_send.at[0, k], halo_recv.at[0, k],
            device_id=after, device_id_type=MESH,
        )
        down = pltpu.make_async_remote_copy(
            press.at[k], halo_hi.at[k], halo_send.at[1, k], halo_recv.at[1, k],
            device_id=before, device_id_type=MESH,
        )
        return up, down

    tx_copy = pltpu.make_async_remote_copy(
        tx_h.at[0], west, tx_send, tx_recv, device_id=after, device_id_type=MESH
    )

    def start_halo(k):
        up, down = halo_copies(k)

        @pl.when(jnp.logical_not(last))
        def _():
            up.start()

        @pl.when(jnp.logical_not(first))
        def _():
            down.start()

    def wait_halo(k):
        up, down = halo_copies(k)

        @pl.when(jnp.logical_not(first))
        def _():
            up.wait_recv()

        @pl.when(jnp.logical_not(last))
        def _():
            down.wait_recv()

    def wait_halo_send(k):
        up, down = halo_copies(k)

        @pl.when(jnp.logical_not(last))
        def _():
            up.wait_send()

        @pl.when(jnp.logical_not(first))
        def _():
            down.wait_send()

    def lanes(values):
        out = jnp.zeros((1, 128), F32)
        for j, v in enumerate(values):
            out = jnp.where(lane == j, v, out)
        return out

    def block_sums(k):
        p = press[k]
        return [total(wells[b] * p) for b in range(BLOCKS)]

    def start_gather(k):
        src = msg0 if k == 0 else msg.at[k - 1]
        dst = ag0 if k == 0 else ag.at[k - 1]

        def send(i, carry):
            pltpu.make_async_remote_copy(
                src, dst.at[f], ag_send.at[k], ag_recv.at[k],
                device_id=flow_dev(lax.rem(f + i, NF)), device_id_type=MESH,
            ).start()
            return carry

        lax.fori_loop(1, NF, send, 0)

    def gather_wait(k, sem):
        dst = ag0 if k == 0 else ag.at[k - 1]
        part = dst.at[pl.ds(0, NF - 1)]
        pltpu.make_async_copy(part, part, sem).wait()

    @pl.when(jnp.logical_not(last))
    def _():
        tx_copy.start()

    start_halo(0)
    well_ids = [well_ref[b : b + 1, :].astype(F32) for b in range(BLOCKS)]
    msg0[:, 0:128] = lanes(block_sums(0))
    msg0[:, 128:256] = lanes(weight_sums)
    msg0[:, 256:384] = jnp.where(lane < BLOCKS, lanes(well_ids), -1.0)
    ag0[f] = msg0[...]
    start_gather(0)

    has_lo, has_hi = d > 0, d < ND - 1

    def y_copies(up):
        target = (g, lax.rem(d + 1, ND)) if up else (g, lax.rem(d + ND - 1, ND))
        at = 0 if up else 2 * YS
        s = 0 if up else 1
        return (
            pltpu.make_async_remote_copy(
                u_h, ua.at[:, pl.ds(HALO, XS), pl.ds(at, YS)], usend.at[s, 0], urecv.at[s, 0],
                device_id=target, device_id_type=MESH,
            ),
            pltpu.make_async_remote_copy(
                mod_h, mod.at[pl.ds(HALO, XS), pl.ds(at, YS)], usend.at[s, 1], urecv.at[s, 1],
                device_id=target, device_id_type=MESH,
            ),
        )

    def x_copies(up):
        target = (lax.rem(g + 1, NG), d) if up else (lax.rem(g + NG - 1, NG), d)
        src = XS if up else HALO
        dst = 0 if up else HALO + XS
        s = 0 if up else 1
        return (
            pltpu.make_async_remote_copy(
                ua.at[:, pl.ds(src, HALO)], ua.at[:, pl.ds(dst, HALO)], xsend.at[s, 0], xrecv.at[s, 0],
                device_id=target, device_id_type=MESH,
            ),
            pltpu.make_async_remote_copy(
                mod.at[pl.ds(src, HALO)], mod.at[pl.ds(dst, HALO)], xsend.at[s, 1], xrecv.at[s, 1],
                device_id=target, device_id_type=MESH,
            ),
        )

    @pl.when(has_hi)
    def _():
        for c in y_copies(True):
            c.start()

    @pl.when(has_lo)
    def _():
        for c in y_copies(False):
            c.start()

    p0 = press[0]
    storage = rdiag[...]
    base[...] = storage * p0 - BIOT * base[...]
    east[...] = jnp.where(last, 0.0, east[...])
    north[...] = jnp.where(iota((NY, NZ), 0) == NY - 1, 0.0, north[...])
    south[...] = prev_y(north[...])
    upper[...] = jnp.where(iota((NY, NZ), 1) == NZ - 1, 0.0, upper[...])
    lower[...] = pltpu.roll(upper[...], 1, 1)
    partial_sum = storage + east[...] + north[...] + south[...] + upper[...] + lower[...]
    for b in range(BLOCKS):
        partial_sum = partial_sum + wells[b]
    rdiag[...] = partial_sum

    rates, strengths = [], []
    for k in range(FLOW_SWEEPS):
        if k == 0:

            @pl.when(jnp.logical_not(first))
            def _():
                tx_copy.wait_recv()

            rdiag[...] = 1.0 / (rdiag[...] + west[...])
        gather_wait(k, ag_recv.at[k])
        if k == 0:
            ids = ag0[:, :, 256:384]
            parts = ag0[:, :, 128:256]
            sums = ag0[:, :, 0:128]
            rate_at = iota((1, 256), 1)
            for b in range(BLOCKS):
                mask = jnp.where(ids == well_ids[b].reshape(1, 1, 1), 1.0, 0.0)
                masks[b] = mask
                strengths.append(total(jnp.sum(mask * parts, axis=0)))
                rates.append(
                    jnp.sum(
                        jnp.where(rate_at == well_ref[b : b + 1, :], rate_ref[...], 0.0),
                        axis=1,
                        keepdims=True,
                    )
                )
        else:
            sums = ag[k - 1]
        bottoms = [
            (rates[b] + total(jnp.sum(masks[b] * sums, axis=0))) / strengths[b]
            for b in range(BLOCKS)
        ]
        wait_halo(k)
        p = press[k]
        acc = base[...] + east[...] * halo_hi[k] + west[...] * halo_lo[k]
        acc = acc + north[...] * next_y(p) + south[...] * prev_y(p)
        acc = acc + upper[...] * pltpu.roll(p, NZ - 1, 1) + lower[...] * pltpu.roll(p, 1, 1)
        for b in range(BLOCKS):
            acc = acc + wells[b] * bottoms[b]
        new = acc * rdiag[...]
        if k < FLOW_SWEEPS - 1:
            press[k + 1] = new
            start_halo(k + 1)
            row = lanes(block_sums(k + 1))
            msg[k] = row
            ag[k, f] = row
            start_gather(k + 1)
        else:
            ppad[YS : YS + NY, :] = new
        if k == 1:
            @pl.when(has_lo)
            def _():
                for c in y_copies(True):
                    c.wait_recv()

            @pl.when(has_hi)
            def _():
                for c in y_copies(False):
                    c.wait_recv()

            own_u.wait()
            own_m.wait()

            @pl.when(g < NG - 1)
            def _():
                for c in x_copies(True):
                    c.start()

            @pl.when(g > 0)
            def _():
                for c in x_copies(False):
                    c.start()

    p_copy = pltpu.make_async_copy(ppad.at[pl.ds(YS, NY)], p_out.at[0], out_sem.at[0])
    p_copy.start()

    def window(t):
        return ppad.at[pl.ds(pl.multiple_of(t * YS, YS), YW)]

    own_window = pltpu.make_async_copy(window(d), pwin.at[HALO + d], pw_self)
    own_window.start()

    def send_own(i, carry):
        t = lax.rem(d + i, ND)
        pltpu.make_async_remote_copy(
            window(t), pwin.at[HALO + d], pw_send.at[0], pw_recv.at[0],
            device_id=(g, t), device_id_type=MESH,
        ).start()
        return carry

    lax.fori_loop(1, ND, send_own, 0)
    to_hi = jnp.logical_and(d >= XS - HALO, g < NG - 1)
    to_lo = jnp.logical_and(d < HALO, g > 0)

    @pl.when(to_hi)
    def _():
        def send(i, carry):
            t = lax.rem(d + i, ND)
            pltpu.make_async_remote_copy(
                window(t), pwin.at[d - (XS - HALO)], pw_send.at[1], pw_recv.at[1],
                device_id=(g + 1, t), device_id_type=MESH,
            ).start()
            return carry

        lax.fori_loop(0, ND, send, 0)

    @pl.when(to_lo)
    def _():
        def send(i, carry):
            t = lax.rem(d + i, ND)
            pltpu.make_async_remote_copy(
                window(t), pwin.at[HALO + XS + d], pw_send.at[2], pw_recv.at[2],
                device_id=(g - 1, t), device_id_type=MESH,
            ).start()
            return carry

        lax.fori_loop(0, ND, send, 0)

    def window_wait(count, sem):
        part = pwin.at[pl.ds(0, count)]
        pltpu.make_async_copy(part, part, sem).wait()

    @pl.when(g > 0)
    def _():
        for c in x_copies(True):
            c.wait_recv()

    @pl.when(g < NG - 1)
    def _():
        for c in x_copies(False):
            c.wait_recv()

    @pl.when(g < NG - 1)
    def _():
        for c in x_copies(True):
            c.wait_send()

    @pl.when(g > 0)
    def _():
        for c in x_copies(False):
            c.wait_send()

    row_y = iota((YW, NZ), 0) + (d - 1) * YS
    inside_y = jnp.logical_and(row_y >= 0, row_y < NY)

    def inside(i):
        x = g * XS - HALO + i
        return jnp.logical_and(inside_y, jnp.logical_and(x >= 0, x < NG * XS))

    def scale_plane(i, carry):
        gain[i] = jnp.where(inside(i), (-0.5 * BIOT * RELAX / 26.0), 0.0) / mod[i]
        return carry

    lax.fori_loop(1, XW - 1, scale_plane, 0)

    own_window.wait()
    window_wait(ND - 1, pw_recv.at[0])

    @pl.when(g > 0)
    def _():
        window_wait(HALO, pw_recv.at[1])

    @pl.when(g < NG - 1)
    def _():
        window_wait(HALO, pw_recv.at[2])

    def force_plane(i, carry):
        p = pwin[i]
        r = gain[i]
        force[0, i] = r * (pwin[i + 1] - pwin[i - 1])
        force[1, i] = r * (next_y(p) - prev_y(p))
        force[2, i] = r * (next_z(p) - prev_z(p))
        return carry

    lax.fori_loop(1, XW - 1, force_plane, 0)

    def z_stage(src, i):
        for c in range(3):
            v = src[c, i]
            hi, lo = next_z(v), prev_z(v)
            tzb[c, i] = v + hi + lo
            dzb[c, i] = hi - lo

    for s in range(MECH_SWEEPS):
        src, dst = (ua, ub) if s % 2 == 0 else (ub, ua)
        z_stage(src, s)
        z_stage(src, s + 1)

        def mech_plane(i, carry, src=src, dst=dst):
            z_stage(src, i + 1)
            ok = inside(i)
            alpha = jnp.where(ok, ALPHA, 0.0)
            beta = jnp.where(ok, BETA, 0.0)
            e = [
                COUPLE * (src[1, i + 1] - src[1, i - 1]),
                COUPLE * (src[0, i + 1] - src[0, i - 1] + dzb[2, i]),
                COUPLE * dzb[1, i],
            ]
            extra = [
                COUPLE * (dzb[2, i + 1] - dzb[2, i - 1]),
                None,
                COUPLE * (dzb[0, i + 1] - dzb[0, i - 1]),
            ]
            for c in range(3):
                box = tzb[c, i - 1] + tzb[c, i] + tzb[c, i + 1]
                r = box + next_y(box + e[c]) + prev_y(box - e[c])
                if extra[c] is not None:
                    r = r + extra[c]
                dst[c, i] = alpha * src[c, i] + beta * r + force[c, i]
            return carry

        lax.fori_loop(s + 1, XW - 1 - s, mech_plane, 0)

    final = ua if MECH_SWEEPS % 2 == 0 else ub
    u_copy = pltpu.make_async_copy(
        final.at[:, pl.ds(HALO, XS), pl.ds(YS, YS)], u_out, out_sem.at[1]
    )
    u_copy.start()

    rows = pl.ds(pl.multiple_of(d * YS, YS), YS)

    def strain_plane(i, carry):
        t = lax.rem(d + i, ND)
        x = t + HALO
        uy = final[1, x]
        uz = final[2, x, YS : 2 * YS, :]
        dx = final[0, x + 1, YS : 2 * YS, :] - final[0, x - 1, YS : 2 * YS, :]
        dy = (next_y(uy) - prev_y(uy))[YS : 2 * YS, :]
        strain[t] = 0.5 * (dx + dy + next_z(uz) - prev_z(uz))

        @pl.when(i > 0)
        def _():
            pltpu.make_async_remote_copy(
                strain.at[t], s_out.at[0, rows], st_send, st_recv,
                device_id=(g, t), device_id_type=MESH,
            ).start()

        return carry

    lax.fori_loop(0, ND, strain_plane, 0)
    own_strain = pltpu.make_async_copy(strain.at[d], s_out.at[0, rows], st_self)
    own_strain.start()

    @pl.when(jnp.logical_not(last))
    def _():
        tx_copy.wait_send()

    for k in range(FLOW_SWEEPS):
        wait_halo_send(k)
        gather_wait(k, ag_send.at[k])

    @pl.when(has_hi)
    def _():
        for c in y_copies(True):
            c.wait_send()

    @pl.when(has_lo)
    def _():
        for c in y_copies(False):
            c.wait_send()

    window_wait(ND - 1, pw_send.at[0])

    @pl.when(to_hi)
    def _():
        window_wait(ND, pw_send.at[1])

    @pl.when(to_lo)
    def _():
        window_wait(ND, pw_send.at[2])

    p_copy.wait()
    u_copy.wait()
    own_strain.wait()
    part = strain.at[pl.ds(0, ND - 1)]
    pltpu.make_async_copy(part, part, st_send).wait()
    pltpu.make_async_copy(part, part, st_recv).wait()


def body(
    pressure_old, strain_change, storage, trans_x, trans_y, trans_z, displacement_old, modulus,
    perf_cell, perf_well, perf_count, perf_index, well_rate,
):
    dma = pltpu.SemaphoreType.DMA
    vmem = lambda *shape: pltpu.VMEM(shape, F32)
    plane = (NY, NZ)
    window = (XW, YW, NZ)
    hbm = pl.BlockSpec(memory_space=pl.ANY)
    local = pl.BlockSpec(memory_space=pltpu.VMEM)
    return pl.pallas_call(
        kernel,
        name="poro_step",
        out_shape=(
            jax.ShapeDtypeStruct((1, NY, NZ), F32),
            jax.ShapeDtypeStruct((3, XS, YS, NZ), F32),
            jax.ShapeDtypeStruct((1, NY, NZ), F32),
        ),
        in_specs=[hbm] * 8 + [local] * 5,
        out_specs=(hbm, hbm, hbm),
        scratch_shapes=[
            vmem(FLOW_SWEEPS, *plane),
            vmem(*plane),
            vmem(*plane),
            vmem(*plane),
            vmem(*plane),
            vmem(*plane),
            vmem(*plane),
            vmem(*plane),
            vmem(*plane),
            vmem(BLOCKS, *plane),
            vmem(FLOW_SWEEPS, *plane),
            vmem(FLOW_SWEEPS, *plane),
            vmem(1, 384),
            vmem(FLOW_SWEEPS - 1, 1, 128),
            vmem(NF, 1, 384),
            vmem(FLOW_SWEEPS - 1, NF, 1, 128),
            vmem(BLOCKS, NF, 1, 128),
            vmem(NY + 2 * YS, NZ),
            vmem(*window),
            vmem(3, *window),
            vmem(3, *window),
            vmem(*window),
            vmem(*window),
            vmem(3, *window),
            vmem(3, *window),
            vmem(3, *window),
            vmem(XS, YS, NZ),
            dma((6,)),
            dma((2,)),
            dma((2, FLOW_SWEEPS)),
            dma((2, FLOW_SWEEPS)),
            dma,
            dma,
            dma((FLOW_SWEEPS,)),
            dma((FLOW_SWEEPS,)),
            dma((2, 2)),
            dma((2, 2)),
            dma((2, 2)),
            dma((2, 2)),
            dma((3,)),
            dma((3,)),
            dma,
            dma,
            dma,
            dma,
            dma((2,)),
        ],
        compiler_params=pltpu.CompilerParams(
            collective_id=0, has_side_effects=True, vmem_limit_bytes=48 << 20
        ),
    )(
        pressure_old, strain_change, storage, trans_x, trans_y, trans_z, displacement_old, modulus,
        perf_cell, perf_well.reshape(BLOCKS, 1), perf_count.reshape(BLOCKS, 1), perf_index,
        well_rate.reshape(1, -1),
    )


def solution(mesh):
    flow = P(("grp", "dev"), None, None)
    slabs = P(None, "grp", "dev", None)
    return jax.shard_map(
        body,
        mesh=mesh,
        in_specs=(
            flow, flow, flow, flow, flow, flow, slabs, P("grp", "dev", None),
            P(("grp", "dev"), None), P(("grp", "dev")), P(("grp", "dev")), P(("grp", "dev"), None), P(),
        ),
        out_specs=(flow, slabs, flow),
        check_vma=False,
    )
```

```python
import functools

import jax
import jax.numpy as jnp
from jax import lax
from jax.experimental import pallas as pl
from jax.experimental.pallas import tpu as pltpu
from jax.sharding import PartitionSpec as P

MESH = pl.DeviceIdType.MESH
F32 = jnp.float32

FLOW_SWEEPS = 4
MECH_SWEEPS = 6
BIOT = 0.8
RELAX = 0.6
COUPLE = 0.375

NG, ND = 4, 32
NF = NG * ND
NY, NZ = 256, 256
XS, YS = 32, 8
HALO = MECH_SWEEPS + 1
CH, SL = 8, 6
XW = CH * SL
YW = 3 * YS
BLOCKS = 4

ALPHA = 1.0 - RELAX * 27.0 / 26.0
BETA = RELAX / 26.0


def iota(shape, dim):
    return lax.broadcasted_iota(jnp.int32, shape, dim)


def next_z(v):
    n = v.shape[-1]
    return jnp.where(iota(v.shape, 1) == n - 1, 0.0, pltpu.roll(v, n - 1, 1))


def prev_z(v):
    return jnp.where(iota(v.shape, 1) == 0, 0.0, pltpu.roll(v, 1, 1))


def next_y(v):
    return pltpu.roll(v, v.shape[0] - 1, 0)


def prev_y(v):
    return pltpu.roll(v, 1, 0)


def extend(slots):
    return [pltpu.roll(slots[-1], 1, 0)] + slots + [pltpu.roll(slots[0], CH - 1, 0)]


def total(v):
    return jnp.sum(jnp.sum(v, axis=0, keepdims=True), axis=1, keepdims=True)


def kernel(
    p0_h, sc_h, st_h, tx_h, ty_h, tz_h, u_h, mod_h, cell_h, well_h, cnt_h, idx_h, rate_h,
    p_out, u_out, s_out,
    cell_ref, well_ref, cnt_ref, idx_ref, rate_ref,
    press, base, east, west, north, south, upper, lower, rdiag, wells, halo_lo, halo_hi,
    msg, ag0, ag, masks,
    ppad, nat, pwin, ua, ub, gain, force, xsum, shear, dy_z, dz_z, dx_z, betas, strain,
    small_sem, load_sem, uload_sem, halo_send, halo_recv, tx_send, tx_recv, ag_send, ag_recv,
    usend, urecv, xsend, xrecv, relay_sem, pw_send, pw_recv, pw_self, st_send, st_recv, st_self,
    out_sem,
):
    g = lax.axis_index("grp")
    d = lax.axis_index("dev")
    f = g * ND + d
    first, last = f == 0, f == NF - 1
    has_lo, has_hi = d > 0, d < ND - 1
    has_west, has_east = g > 0, g < NG - 1

    def flow_dev(k):
        return (k // ND, lax.rem(k, ND))

    after, before = flow_dev(lax.rem(f + 1, NF)), flow_dev(lax.rem(f + NF - 1, NF))

    small_loads = [
        pltpu.make_async_copy(src, dst, small_sem.at[i])
        for i, (src, dst) in enumerate(
            [
                (cell_h, cell_ref),
                (well_h, well_ref),
                (cnt_h, cnt_ref),
                (idx_h, idx_ref),
                (rate_h, rate_ref),
            ]
        )
    ]
    plane_loads = [
        pltpu.make_async_copy(src.at[0], dst, load_sem.at[i])
        for i, (src, dst) in enumerate(
            [
                (p0_h, press.at[0]),
                (sc_h, base),
                (st_h, rdiag),
                (tx_h, east),
                (ty_h, north),
                (tz_h, upper),
            ]
        )
    ]
    own_u = pltpu.make_async_copy(
        u_h, nat.at[pl.ds(0, 3), pl.ds(HALO, XS), pl.ds(YS, YS)], uload_sem.at[0]
    )
    own_m = pltpu.make_async_copy(
        mod_h, nat.at[3, pl.ds(HALO, XS), pl.ds(YS, YS)], uload_sem.at[1]
    )
    for c in small_loads + plane_loads + [own_u, own_m]:
        c.start()

    def fill(planes, rows):
        n, m = planes.stop - planes.start, rows.stop - rows.start
        nat[0:3, planes, rows, :] = jnp.zeros((3, n, m, NZ), F32)
        nat[3, planes, rows, :] = jnp.ones((n, m, NZ), F32)

    own_planes, all_rows = slice(HALO, HALO + XS), slice(0, YW)
    fill(slice(2 * HALO + XS, XW), all_rows)
    pwin[...] = jnp.zeros(pwin.shape, F32)

    @pl.when(d == 0)
    def _():
        fill(own_planes, slice(0, YS))

    @pl.when(d == ND - 1)
    def _():
        fill(own_planes, slice(2 * YS, YW))

    @pl.when(g == 0)
    def _():
        fill(slice(0, HALO), all_rows)

    @pl.when(g == NG - 1)
    def _():
        fill(slice(HALO + XS, 2 * HALO + XS), all_rows)

    barrier = pltpu.get_barrier_semaphore()

    def greet(i, carry):
        pl.semaphore_signal(
            barrier, inc=1, device_id=flow_dev(lax.rem(f + i, NF)), device_id_type=MESH
        )
        return carry

    lax.fori_loop(1, NF, greet, 0)

    @pl.when(first)
    def _():
        halo_lo[...] = jnp.zeros(halo_lo.shape, F32)
        west[...] = jnp.zeros((NY, NZ), F32)

    @pl.when(last)
    def _():
        halo_hi[...] = jnp.zeros(halo_hi.shape, F32)

    ppad[0:YS, :] = jnp.zeros((YS, NZ), F32)
    ppad[NY + YS :, :] = jnp.zeros((YS, NZ), F32)
    for i in range(SL):
        x = iota((CH, NZ), 0) * SL + i + g * XS - HALO
        betas[i] = jnp.where(jnp.logical_and(x >= 0, x < NG * XS), BETA, 0.0)

    for c in small_loads:
        c.wait()
    lane = iota((1, 128), 1)
    weight_sums = []
    for b in range(BLOCKS):
        live = lane < cnt_ref[b]
        weight = jnp.where(live, idx_ref[b : b + 1, :], 0.0)
        cell = cell_ref[b : b + 1, :]
        row, col = cell // NZ, lax.rem(cell, NZ)
        at_row = iota((NY, 128), 0) == row
        at_col = jnp.where(iota((NZ, 128), 0) == col, 1.0, 0.0).astype(jnp.bfloat16)
        rest = weight
        plane = jnp.zeros((NY, NZ), F32)
        for _ in range(3):
            part = rest.astype(jnp.bfloat16)
            rest = rest - part.astype(F32)
            spread = jnp.where(at_row, part.astype(F32), 0.0).astype(jnp.bfloat16)
            plane = plane + lax.dot_general(
                spread, at_col, (((1,), (1,)), ((), ())), preferred_element_type=F32
            )
        wells[b] = plane
        weight_sums.append(jnp.sum(weight, axis=1, keepdims=True))

    for c in plane_loads:
        c.wait()

    def halo_copies(k):
        up = pltpu.make_async_remote_copy(
            press.at[k], halo_lo.at[k], halo_send.at[0, k], halo_recv.at[0, k],
            device_id=after, device_id_type=MESH,
        )
        down = pltpu.make_async_remote_copy(
            press.at[k], halo_hi.at[k], halo_send.at[1, k], halo_recv.at[1, k],
            device_id=before, device_id_type=MESH,
        )
        return up, down

    tx_copy = pltpu.make_async_remote_copy(
        tx_h.at[0], west, tx_send, tx_recv, device_id=after, device_id_type=MESH
    )

    def start_halo(k):
        up, down = halo_copies(k)

        @pl.when(jnp.logical_not(last))
        def _():
            up.start()

        @pl.when(jnp.logical_not(first))
        def _():
            down.start()

    def wait_halo(k):
        up, down = halo_copies(k)

        @pl.when(jnp.logical_not(first))
        def _():
            up.wait_recv()

        @pl.when(jnp.logical_not(last))
        def _():
            down.wait_recv()

    def wait_halo_send(k):
        up, down = halo_copies(k)

        @pl.when(jnp.logical_not(last))
        def _():
            up.wait_send()

        @pl.when(jnp.logical_not(first))
        def _():
            down.wait_send()

    def lanes(values):
        out = jnp.zeros((1, 128), F32)
        for j, v in enumerate(values):
            out = jnp.where(lane == j, v, out)
        return out

    def block_sums(p):
        return lanes([total(wells[b] * p) for b in range(BLOCKS)])

    core, z_lo = lax.rem(g, 2), g // 2
    z_hi, phys_x, phys_y = d // 16, lax.rem(d // 4, 4), lax.rem(d, 4)
    spots = sorted(
        ((x, y) for x in range(4) for y in range(4)),
        key=lambda o: -(min(o[0], 4 - o[0]) + min(o[1], 4 - o[1])),
    )

    def gather_refs(k):
        if k == 0:
            return msg.at[pl.ds(0, 3), pl.ds(0, 1)], lambda r, n: ag0.at[:, pl.ds(r, n)]
        return msg.at[2 + k, pl.ds(0, 1)], lambda r, n: ag.at[k - 1, pl.ds(r, n)]

    def start_gather(k):
        src, dst = gather_refs(k)
        for ox, oy in spots:
            x, y = lax.rem(phys_x + ox, 4), lax.rem(phys_y + oy, 4)

            def send(i, carry, x=x, y=y):
                j = 7 - i
                zh = lax.rem(z_hi + j // 4, 2)
                zl = lax.rem(z_lo + lax.rem(j // 2, 2), 2)
                c = lax.rem(core + lax.rem(j, 2), 2)
                pltpu.make_async_remote_copy(
                    src, dst(f, 1), ag_send.at[k], ag_recv.at[k],
                    device_id=(zl * 2 + c, zh * 16 + x * 4 + y), device_id_type=MESH,
                ).start()
                return carry

            lax.fori_loop(0, 7 if ox == 0 and oy == 0 else 8, send, 0)

    def gather_wait(k, sem):
        part = gather_refs(k)[1](0, NF - 1)
        pltpu.make_async_copy(part, part, sem).wait()

    def y_copies(a):
        src = mod_h if a == 3 else u_h.at[a]
        out = []
        for s, (k, at) in enumerate([(lax.rem(d + 1, ND), 0), (lax.rem(d + ND - 1, ND), 2 * YS)]):
            out.append(
                pltpu.make_async_remote_copy(
                    src, nat.at[a, pl.ds(HALO, XS), pl.ds(at, YS)],
                    usend.at[s, a], urecv.at[s, a], device_id=(g, k), device_id_type=MESH,
                )
            )
        return out

    def x_copies(a):
        out = []
        for s, (k, at, to) in enumerate(
            [(lax.rem(g + 1, NG), XS, 0), (lax.rem(g + NG - 1, NG), HALO, HALO + XS)]
        ):
            out.append(
                pltpu.make_async_remote_copy(
                    nat.at[a, pl.ds(at, HALO)], nat.at[a, pl.ds(to, HALO)],
                    xsend.at[s, a], xrecv.at[s, a], device_id=(k, d), device_id_type=MESH,
                )
            )
        return out

    def start_pair(copies, to_up, to_down):
        @pl.when(to_up)
        def _():
            copies[0].start()

        @pl.when(to_down)
        def _():
            copies[1].start()

    def recv_pair(copies, to_up, to_down):
        @pl.when(to_down)
        def _():
            copies[0].wait_recv()

        @pl.when(to_up)
        def _():
            copies[1].wait_recv()

    def send_pair(copies, to_up, to_down):
        @pl.when(to_up)
        def _():
            copies[0].wait_send()

        @pl.when(to_down)
        def _():
            copies[1].wait_send()

    def pass_on(a):
        recv_pair(y_copies(a), has_hi, has_lo)
        start_pair(x_copies(a), has_east, has_west)

    def relay_copies(a):
        dst = gain if a == 3 else ua.at[a]
        return [
            pltpu.make_async_copy(
                nat.at[a, pl.ds(c * SL, SL)], dst.at[:, :, c], relay_sem.at[a, c]
            )
            for c in range(CH)
        ]

    def relay(a):
        recv_pair(x_copies(a), has_east, has_west)
        send_pair(x_copies(a), has_east, has_west)
        for c in relay_copies(a):
            c.start()

    pl.semaphore_wait(barrier, NF - 1)

    @pl.when(jnp.logical_not(last))
    def _():
        tx_copy.start()

    start_halo(0)
    well_ids = [well_ref[b].astype(F32) for b in range(BLOCKS)]
    msg[0, 0:1] = block_sums(press[0])
    msg[1, 0:1] = lanes(weight_sums)
    msg[2, 0:1] = jnp.where(lane < BLOCKS, lanes(well_ids), -1.0)
    for j in range(3):
        ag0[j, pl.ds(f, 1), :] = msg[j, 0:1]
    start_gather(0)
    start_pair(y_copies(3), has_hi, has_lo)

    p0 = press[0]
    storage = rdiag[...]
    base[...] = storage * p0 - BIOT * base[...]
    east[...] = jnp.where(last, 0.0, east[...])
    north[...] = jnp.where(iota((NY, NZ), 0) == NY - 1, 0.0, north[...])
    south[...] = prev_y(north[...])
    upper[...] = jnp.where(iota((NY, NZ), 1) == NZ - 1, 0.0, upper[...])
    lower[...] = pltpu.roll(upper[...], 1, 1)
    partial_sum = storage + east[...] + north[...] + south[...] + upper[...] + lower[...]
    for b in range(BLOCKS):
        partial_sum = partial_sum + wells[b]
    rdiag[...] = partial_sum
    own_u.wait()
    own_m.wait()

    rates, strengths = [], []
    for k in range(FLOW_SWEEPS):
        if k == 0:

            @pl.when(jnp.logical_not(first))
            def _():
                tx_copy.wait_recv()

            rdiag[...] = 1.0 / (rdiag[...] + west[...])
        wait_halo(k)
        order = [3, 0, 1, 2]
        pass_on(order[k])
        if k < 3:
            start_pair(y_copies(order[k + 1]), has_hi, has_lo)
        if k > 0:
            relay(order[k - 1])
        gather_wait(k, ag_recv.at[k])
        if k == 0:
            sums = ag0[0]
            rate_at = iota((1, 256), 1)
            for b in range(BLOCKS):
                mask = jnp.where(ag0[2] == well_ids[b], 1.0, 0.0)
                masks[b] = mask
                strengths.append(total(mask * ag0[1]))
                rates.append(
                    jnp.sum(
                        jnp.where(rate_at == well_ref[b], rate_ref[...], 0.0),
                        axis=1,
                        keepdims=True,
                    )
                )
        else:
            sums = ag[k - 1]
        bottoms = [(rates[b] + total(masks[b] * sums)) / strengths[b] for b in range(BLOCKS)]
        p = press[k]
        acc = base[...] + east[...] * halo_hi[k] + west[...] * halo_lo[k]
        acc = acc + north[...] * next_y(p) + south[...] * prev_y(p)
        acc = acc + upper[...] * pltpu.roll(p, NZ - 1, 1) + lower[...] * pltpu.roll(p, 1, 1)
        for b in range(BLOCKS):
            acc = acc + wells[b] * bottoms[b]
        new = acc * rdiag[...]
        if k < FLOW_SWEEPS - 1:
            press[k + 1] = new
            start_halo(k + 1)
            row = block_sums(new)
            msg[3 + k, 0:1] = row
            ag[k, pl.ds(f, 1), :] = row
            start_gather(k + 1)
        else:
            ppad[YS : YS + NY, :] = new

    def window(t):
        return ppad.at[pl.ds(pl.multiple_of(t * YS, YS), YW)]

    def place(x):
        return pwin.at[lax.rem(x, SL), :, x // SL]

    own_window = pltpu.make_async_copy(window(d), place(HALO + d), pw_self)
    own_window.start()

    def spread(first_step, x, target, j):
        def send(i, carry):
            t = lax.rem(d + i, ND)
            pltpu.make_async_remote_copy(
                window(t), place(x), pw_send.at[j], pw_recv.at[j],
                device_id=(target, t), device_id_type=MESH,
            ).start()
            return carry

        lax.fori_loop(first_step, ND, send, 0)

    spread(1, HALO + d, g, 0)
    to_hi = jnp.logical_and(d >= XS - HALO, has_east)
    to_lo = jnp.logical_and(d < HALO, has_west)

    @pl.when(to_hi)
    def _():
        spread(0, d - (XS - HALO), g + 1, 1)

    @pl.when(to_lo)
    def _():
        spread(0, HALO + XS + d, g - 1, 2)

    p_copy = pltpu.make_async_copy(ppad.at[pl.ds(YS, NY)], p_out.at[0], out_sem.at[0])
    p_copy.start()

    def window_wait(count, sem):
        part = nat.at[0, pl.ds(0, count)]
        pltpu.make_async_copy(part, part, sem).wait()

    relay(2)
    for c in relay_copies(3):
        c.wait()

    def gain_row(y, carry):
        gy = (d - 1) * YS + y
        inside = jnp.logical_and(gy >= 0, gy < NY)
        scale = jnp.where(inside, -0.5 * BIOT / BETA * RELAX / 26.0, 0.0)
        for i in range(SL):
            gain[i, y] = scale * betas[i] / gain[i, y]
        return carry

    lax.fori_loop(2, YW - 2, gain_row, 0)
    for a in range(3):
        for c in relay_copies(a):
            c.wait()

    own_window.wait()
    window_wait(ND - 1, pw_recv.at[0])

    @pl.when(has_west)
    def _():
        window_wait(HALO, pw_recv.at[1])

    @pl.when(has_east)
    def _():
        window_wait(HALO, pw_recv.at[2])

    def force_row(y, carry):
        p = extend([pwin[i, y] for i in range(SL)])
        for i in range(SL):
            r = gain[i, y]
            force[0, i, y] = r * (p[i + 2] - p[i])
            force[1, i, y] = r * (pwin[i, y + 1] - pwin[i, y - 1])
            force[2, i, y] = r * (next_z(p[i + 1]) - prev_z(p[i + 1]))
        return carry

    lax.fori_loop(2, YW - 2, force_row, 0)

    for s in range(MECH_SWEEPS):
        src, dst = (ua, ub) if s % 2 == 0 else (ub, ua)
        y0, y1 = 2 + s, YW - 2 - s

        def row_values(y, src=src):
            tz, dz = [], []
            for c in range(3):
                t, q = [], []
                for i in range(SL):
                    v = src[c, i, y]
                    hi, lo = next_z(v), prev_z(v)
                    t.append(v + hi + lo)
                    q.append(hi - lo)
                tz.append(extend(t))
                dz.append(q)
            sums = []
            for t in tz:
                r = []
                for i in range(0, SL, 2):
                    pair = t[i + 1] + t[i + 2]
                    r += [t[i] + pair, pair + t[i + 3]]
                sums.append(r)
            ux = extend([src[0, i, y] for i in range(SL)])
            dx = extend(dz[0])
            along_y = [ux[i + 2] - ux[i] + dz[2][i] for i in range(SL)]
            cross = [dx[i + 2] - dx[i] for i in range(SL)]
            return sums, along_y, dz[1], dz[2], cross

        def row_store(y, values):
            sums, along_y, dzy, dzz, cross = values
            for i in range(SL):
                for c in range(3):
                    xsum[c, i, y] = sums[c][i]
                shear[i, y] = along_y[i]
                dy_z[i, y] = dzy[i]
                dz_z[i, y] = dzz[i]
                dx_z[i, y] = cross[i]

        def combine(y, src=src, dst=dst):
            gy = (d - 1) * YS + y
            inside = jnp.logical_and(gy >= 0, gy < NY).astype(F32)
            along_x = extend([src[1, i, y + 1] - src[1, i, y - 1] + dz_z[i, y] for i in range(SL)])
            for i in range(SL):
                beta = betas[i] * inside
                mixed = [
                    along_x[i + 2] - along_x[i],
                    shear[i, y + 1] - shear[i, y - 1],
                    dx_z[i, y] + dy_z[i, y + 1] - dy_z[i, y - 1],
                ]
                for c in range(3):
                    box = xsum[c, i, y - 1] + xsum[c, i, y] + xsum[c, i, y + 1]
                    r = box + COUPLE * mixed[c] + (ALPHA / BETA) * src[c, i, y]
                    dst[c, i, y] = beta * r + force[c, i, y]

        for y in (y0 - 1, y0, y0 + 1):
            row_store(y, row_values(y))

        def mech_row(y, carry, y1=y1):
            ahead = jnp.minimum(y + 2, y1)
            values = row_values(ahead)
            combine(y)
            row_store(ahead, values)
            return carry

        lax.fori_loop(y0, y1, mech_row, 0, unroll=2)

    final = ua if MECH_SWEEPS % 2 == 0 else ub

    def strain_row(y, carry):
        ux = extend([final[0, i, y] for i in range(SL)])
        for i in range(SL):
            uz = final[2, i, y]
            div = ux[i + 2] - ux[i] + final[1, i, y + 1] - final[1, i, y - 1]
            strain[i, y - YS] = 0.5 * (div + next_z(uz) - prev_z(uz))
        return carry

    lax.fori_loop(YS, 2 * YS, strain_row, 0)
    rows = pl.ds(pl.multiple_of(d * YS, YS), YS)

    def strain_of(t):
        x = t + HALO
        return strain.at[lax.rem(x, SL), :, x // SL]

    def send_strain(i, carry):
        t = lax.rem(d + i, ND)
        pltpu.make_async_remote_copy(
            strain_of(t), s_out.at[0, rows], st_send, st_recv,
            device_id=(g, t), device_id_type=MESH,
        ).start()
        return carry

    lax.fori_loop(1, ND, send_strain, 0)
    own_strain = pltpu.make_async_copy(strain_of(d), s_out.at[0, rows], st_self)
    own_strain.start()
    u_copies = []
    for c in range(CH):
        lo, hi = max(c * SL, HALO), min((c + 1) * SL, HALO + XS)
        if lo < hi:
            u_copies.append(
                pltpu.make_async_copy(
                    final.at[:, pl.ds(lo - c * SL, hi - lo), pl.ds(YS, YS), c],
                    u_out.at[:, pl.ds(lo - HALO, hi - lo)],
                    out_sem.at[1 + c],
                )
            )
    for c in u_copies:
        c.start()

    @pl.when(jnp.logical_not(last))
    def _():
        tx_copy.wait_send()

    for k in range(FLOW_SWEEPS):
        wait_halo_send(k)
        gather_wait(k, ag_send.at[k])
    for a in range(4):
        send_pair(y_copies(a), has_hi, has_lo)
    window_wait(ND - 1, pw_send.at[0])

    @pl.when(to_hi)
    def _():
        window_wait(ND, pw_send.at[1])

    @pl.when(to_lo)
    def _():
        window_wait(ND, pw_send.at[2])

    p_copy.wait()
    for c in u_copies:
        c.wait()
    own_strain.wait()
    part = ppad.at[pl.ds(0, (ND - 1) * YS)]
    pltpu.make_async_copy(part, part, st_send).wait()
    pltpu.make_async_copy(part, part, st_recv).wait()


def body(
    pressure_old, strain_change, storage, trans_x, trans_y, trans_z, displacement_old, modulus,
    perf_cell, perf_well, perf_count, perf_index, well_rate,
):
    dma = pltpu.SemaphoreType.DMA
    vmem = lambda *shape: pltpu.VMEM(shape, F32)
    plane = (NY, NZ)
    slabs = (SL, YW, CH, NZ)
    hbm = pl.BlockSpec(memory_space=pl.ANY)
    return pl.pallas_call(
        kernel,
        name="poro_step",
        out_shape=(
            jax.ShapeDtypeStruct((1, NY, NZ), F32),
            jax.ShapeDtypeStruct((3, XS, YS, NZ), F32),
            jax.ShapeDtypeStruct((1, NY, NZ), F32),
        ),
        in_specs=[hbm] * 13,
        out_specs=(hbm, hbm, hbm),
        scratch_shapes=[
            pltpu.VMEM((BLOCKS, 128), jnp.int32),
            pltpu.SMEM((BLOCKS,), jnp.int32),
            pltpu.SMEM((BLOCKS,), jnp.int32),
            vmem(BLOCKS, 128),
            vmem(1, 256),
            vmem(FLOW_SWEEPS, *plane),
            vmem(*plane),
            vmem(*plane),
            vmem(*plane),
            vmem(*plane),
            vmem(*plane),
            vmem(*plane),
            vmem(*plane),
            vmem(*plane),
            vmem(BLOCKS, *plane),
            vmem(FLOW_SWEEPS, *plane),
            vmem(FLOW_SWEEPS, *plane),
            vmem(3 + FLOW_SWEEPS - 1, 8, 128),
            vmem(3, NF, 128),
            vmem(FLOW_SWEEPS - 1, NF, 128),
            vmem(BLOCKS, NF, 128),
            vmem(NY + 2 * YS, NZ),
            vmem(4, XW, YW, NZ),
            vmem(*slabs),
            vmem(3, *slabs),
            vmem(3, *slabs),
            vmem(*slabs),
            vmem(3, *slabs),
            vmem(3, *slabs),
            vmem(*slabs),
            vmem(*slabs),
            vmem(*slabs),
            vmem(*slabs),
            vmem(SL, CH, NZ),
            vmem(SL, YS, CH, NZ),
            dma((5,)),
            dma((6,)),
            dma((2,)),
            dma((2, FLOW_SWEEPS)),
            dma((2, FLOW_SWEEPS)),
            dma,
            dma,
            dma((FLOW_SWEEPS,)),
            dma((FLOW_SWEEPS,)),
            dma((2, 4)),
            dma((2, 4)),
            dma((2, 4)),
            dma((2, 4)),
            dma((4, CH)),
            dma((3,)),
            dma((3,)),
            dma,
            dma,
            dma,
            dma,
            dma((1 + CH,)),
        ],
        compiler_params=pltpu.CompilerParams(
            collective_id=0, has_side_effects=True, vmem_limit_bytes=62 << 20
        ),
    )(
        pressure_old, strain_change, storage, trans_x, trans_y, trans_z, displacement_old, modulus,
        perf_cell, perf_well, perf_count, perf_index,
        well_rate.reshape(1, -1),
    )


def solution(mesh):
    flow = P(("grp", "dev"), None, None)
    slabs = P(None, "grp", "dev", None)
    return jax.shard_map(
        body,
        mesh=mesh,
        in_specs=(
            flow, flow, flow, flow, flow, flow, slabs, P("grp", "dev", None),
            P(("grp", "dev"), None), P(("grp", "dev")), P(("grp", "dev")), P(("grp", "dev"), None), P(),
        ),
        out_specs=(flow, slabs, flow),
        check_vma=False,
    )
```

```python
import functools

import jax
import jax.numpy as jnp
from jax import lax
from jax.experimental import pallas as pl
from jax.experimental.pallas import tpu as pltpu
from jax.sharding import PartitionSpec as P

MESH = pl.DeviceIdType.MESH
F32 = jnp.float32

FLOW_SWEEPS = 4
MECH_SWEEPS = 6
BIOT = 0.8
RELAX = 0.6
COUPLE = 0.375

NG, ND = 4, 32
NF = NG * ND
CHIPS = NF // 2
NY, NZ = 256, 256
XS, YS = 32, 8
HALO = MECH_SWEEPS + 1
CH, SL = 8, 6
XW = CH * SL
YW = 3 * YS
BLOCKS = 4
PARTS = 2
PR = NY // PARTS

ALPHA = 1.0 - RELAX * 27.0 / 26.0
BETA = RELAX / 26.0


def iota(shape, dim):
    return lax.broadcasted_iota(jnp.int32, shape, dim)


def next_z(v):
    n = v.shape[-1]
    return jnp.where(iota(v.shape, 1) == n - 1, 0.0, pltpu.roll(v, n - 1, 1))


def prev_z(v):
    return jnp.where(iota(v.shape, 1) == 0, 0.0, pltpu.roll(v, 1, 1))


def next_y(v):
    return pltpu.roll(v, v.shape[0] - 1, 0)


def prev_y(v):
    return pltpu.roll(v, 1, 0)


def extend(slots):
    return [pltpu.roll(slots[-1], 1, 0)] + slots + [pltpu.roll(slots[0], CH - 1, 0)]


def total(v):
    return jnp.sum(jnp.sum(v, axis=0, keepdims=True), axis=1, keepdims=True)


def kernel(
    p0_h, sc_h, st_h, tx_h, ty_h, tz_h, u_h, mod_h, cell_h, well_h, cnt_h, idx_h, rate_h,
    p_out, u_out, s_out,
    cell_ref, well_ref, cnt_ref, idx_ref, rate_ref,
    press, field, base, east, west, north, south, upper, lower, rdiag, wells, sinks, near,
    halo_lo, halo_hi, col_hot, near_msg, near_lo, near_hi, msg, other, joint, ag0, ag, masks,
    ppad, nat, pwin, ua, ub, gain, force, xsum, shear, dy_z, dz_z, dx_z, betas, strain,
    small_sem, load_sem, uload_sem, halo_send, halo_recv, tx_send, tx_recv, near_send, near_recv, join_send, join_recv, ag_send, ag_recv,
    usend, urecv, xsend, xrecv, relay_sem, pw_send, pw_recv, pw_self, st_send, st_recv, st_self,
    out_sem,
):
    g = lax.axis_index("grp")
    d = lax.axis_index("dev")
    f = g * ND + d
    first, last = f == 0, f == NF - 1
    has_lo, has_hi = d > 0, d < ND - 1
    has_west, has_east = g > 0, g < NG - 1

    def flow_dev(k):
        return (k // ND, lax.rem(k, ND))

    after, before = flow_dev(lax.rem(f + 1, NF)), flow_dev(lax.rem(f + NF - 1, NF))

    small_loads = [
        pltpu.make_async_copy(src, dst, small_sem.at[i])
        for i, (src, dst) in enumerate(
            [
                (cell_h, cell_ref),
                (well_h, well_ref),
                (cnt_h, cnt_ref),
                (idx_h, idx_ref),
                (rate_h, rate_ref),
            ]
        )
    ]
    plane_loads = [
        pltpu.make_async_copy(src.at[0], dst, load_sem.at[i])
        for i, (src, dst) in enumerate(
            [
                (p0_h, press.at[0]),
                (sc_h, base),
                (st_h, rdiag),
                (tx_h, east),
                (ty_h, north),
                (tz_h, upper),
            ]
        )
    ]
    own_u = pltpu.make_async_copy(
        u_h, nat.at[pl.ds(0, 3), pl.ds(HALO, XS), pl.ds(YS, YS)], uload_sem.at[0]
    )
    own_m = pltpu.make_async_copy(
        mod_h, nat.at[3, pl.ds(HALO, XS), pl.ds(YS, YS)], uload_sem.at[1]
    )
    for c in small_loads + plane_loads + [own_u, own_m]:
        c.start()

    def fill(planes, rows):
        n, m = planes.stop - planes.start, rows.stop - rows.start
        nat[0:3, planes, rows, :] = jnp.zeros((3, n, m, NZ), F32)
        nat[3, planes, rows, :] = jnp.ones((n, m, NZ), F32)

    own_planes, all_rows = slice(HALO, HALO + XS), slice(0, YW)
    fill(slice(2 * HALO + XS, XW), all_rows)
    pwin[...] = jnp.zeros(pwin.shape, F32)

    @pl.when(d == 0)
    def _():
        fill(own_planes, slice(0, YS))

    @pl.when(d == ND - 1)
    def _():
        fill(own_planes, slice(2 * YS, YW))

    @pl.when(g == 0)
    def _():
        fill(slice(0, HALO), all_rows)

    @pl.when(g == NG - 1)
    def _():
        fill(slice(HALO + XS, 2 * HALO + XS), all_rows)

    barrier = pltpu.get_barrier_semaphore()

    core, z_lo = lax.rem(g, 2), g // 2
    z_hi, phys_x, phys_y = d // 16, lax.rem(d // 4, 4), lax.rem(d, 4)
    phys_z = 2 * z_hi + z_lo
    spots = sorted(
        ((x, y) for x in range(4) for y in range(4)),
        key=lambda o: -(min(o[0], 4 - o[0]) + min(o[1], 4 - o[1])),
    )
    for ox, oy in spots:
        x, y = lax.rem(phys_x + ox, 4), lax.rem(phys_y + oy, 4)

        def greet(j, carry, x=x, y=y):
            z = lax.rem(phys_z + lax.rem(2 + 3 * (j // 2), 4), 4)
            c = lax.rem(core + 1 + lax.rem(j, 2), 2)
            pl.semaphore_signal(
                barrier, inc=1, device_id=(lax.rem(z, 2) * 2 + c, (z // 2) * 16 + x * 4 + y),
                device_id_type=MESH,
            )
            return carry

        if ox == 0 and oy == 0:
            lax.fori_loop(0, 5, greet, 0)
            lax.fori_loop(6, 8, greet, 0)
        else:
            lax.fori_loop(0, 8, greet, 0)

    @pl.when(first)
    def _():
        halo_lo[...] = jnp.zeros(halo_lo.shape, F32)
        near_lo[...] = jnp.zeros(near_lo.shape, F32)
        west[...] = jnp.zeros((NY, NZ), F32)

    @pl.when(last)
    def _():
        halo_hi[...] = jnp.zeros(halo_hi.shape, F32)
        near_hi[...] = jnp.zeros(near_hi.shape, F32)

    ppad[0:YS, :] = jnp.zeros((YS, NZ), F32)
    ppad[NY + YS :, :] = jnp.zeros((YS, NZ), F32)
    for i in range(SL):
        x = iota((CH, NZ), 0) * SL + i + g * XS - HALO
        betas[i] = jnp.where(jnp.logical_and(x >= 0, x < NG * XS), BETA, 0.0)

    for c in small_loads:
        c.wait()
    lane = iota((1, 128), 1)

    def hot(shape, index):
        return jnp.where(iota(shape, 0) == index, 1.0, 0.0).astype(jnp.bfloat16)

    def thirds(v):
        out = []
        for _ in range(3):
            part = v.astype(jnp.bfloat16)
            v = v - part.astype(F32)
            out.append(part)
        return out

    def dense(cell, value):
        at_row = iota((NY, 128), 0) == cell // NZ
        at_col = hot((NZ, 128), lax.rem(cell, NZ))
        plane = jnp.zeros((NY, NZ), F32)
        for part in thirds(value):
            spread = jnp.where(at_row, part.astype(F32), 0.0).astype(jnp.bfloat16)
            plane = plane + lax.dot_general(
                spread, at_col, (((1,), (1,)), ((), ())), preferred_element_type=F32
            )
        return plane

    weights = []
    for b in range(BLOCKS):
        weight = jnp.where(lane < cnt_ref[b], idx_ref[b : b + 1, :], 0.0)
        cell = cell_ref[b : b + 1, :]
        wells[b] = dense(cell, weight)
        col_hot[:, b * 128 : (b + 1) * 128] = hot((NZ, 128), lax.rem(cell, NZ))
        near_msg[b : b + 1, :] = cell.astype(F32)
        weights.append(weight)
    weight_sums = [jnp.sum(w, axis=1, keepdims=True) for w in weights]

    for c in plane_loads:
        c.wait()

    def start_pair(copies, to_up, to_down):
        @pl.when(to_up)
        def _():
            copies[0].start()

        @pl.when(to_down)
        def _():
            copies[1].start()

    def recv_pair(copies, to_up, to_down):
        @pl.when(to_down)
        def _():
            copies[0].wait_recv()

        @pl.when(to_up)
        def _():
            copies[1].wait_recv()

    def send_pair(copies, to_up, to_down):
        @pl.when(to_up)
        def _():
            copies[0].wait_send()

        @pl.when(to_down)
        def _():
            copies[1].wait_send()

    def halo_copies(k, j):
        part = pl.ds(j * PR, PR)
        return [
            pltpu.make_async_remote_copy(
                press.at[k, part], buffer.at[k, part], halo_send.at[s, k, j], halo_recv.at[s, k, j],
                device_id=target, device_id_type=MESH,
            )
            for s, (buffer, target) in enumerate([(halo_lo, after), (halo_hi, before)])
        ]

    tx_copy = pltpu.make_async_remote_copy(
        tx_h.at[0], west, tx_send, tx_recv, device_id=after, device_id_type=MESH
    )
    near_copies = [
        pltpu.make_async_remote_copy(
            near_msg, buffer, near_send.at[s], near_recv.at[s], device_id=target, device_id_type=MESH
        )
        for s, (buffer, target) in enumerate([(near_lo, after), (near_hi, before)])
    ]
    to_after, to_before = jnp.logical_not(last), jnp.logical_not(first)

    chip = z_lo * ND + d

    def lanes(values):
        out = jnp.zeros((1, 128), F32)
        for b, v in enumerate(values):
            out = jnp.where(lane == core * BLOCKS + b, v, out)
        return out

    def block_sums(p):
        return lanes([total(wells[b] * p) for b in range(BLOCKS)])

    def rows_of(ref, k):
        return ref.at[pl.ds(0, 3), pl.ds(0, 1)] if k == 0 else ref.at[2 + k, pl.ds(0, 1)]

    def gathered(k, r, n):
        return ag0.at[:, pl.ds(r, n)] if k == 0 else ag.at[k - 1, pl.ds(r, n)]

    def join_copy(k):
        return pltpu.make_async_remote_copy(
            rows_of(msg, k), rows_of(other, k), join_send.at[k], join_recv.at[k],
            device_id=(z_lo * 2 + 1 - core, d), device_id_type=MESH,
        )

    def start_gather(k):
        join_copy(k).wait_recv()
        for j in range(3) if k == 0 else [2 + k]:
            row = msg[j, 0:1] + other[j, 0:1]
            joint[j, 0:1] = row
            if k == 0:
                ag0[j, pl.ds(chip, 1), :] = row
            else:
                ag[k - 1, pl.ds(chip, 1), :] = row

        def send(x, y, oz):
            z = lax.rem(phys_z + oz, 4)
            pltpu.make_async_remote_copy(
                rows_of(joint, k), gathered(k, chip, 1), ag_send.at[k], ag_recv.at[k],
                device_id=(lax.rem(z, 2) * 2 + core, (z // 2) * 16 + x * 4 + y), device_id_type=MESH,
            ).start()

        for ox, oy in spots:
            x, y = lax.rem(phys_x + ox, 4), lax.rem(phys_y + oy, 4)
            if ox == 0 and oy == 0:
                for oz in (2, 1, 3):
                    send(x, y, oz)
            else:

                def step(j, carry, x=x, y=y):
                    send(x, y, lax.rem(2 + 3 * j, 4))
                    return carry

                lax.fori_loop(0, 4, step, 0)

    def gather_wait(k, sem):
        part = gathered(k, 0, CHIPS - 1)
        pltpu.make_async_copy(part, part, sem).wait()

    def y_copies(a, first_plane=0, planes=XS):
        n = HALO - 1 if a == 3 else HALO
        out = []
        for s, (k, at, to) in enumerate(
            [(lax.rem(d + 1, ND), YS - n, YS - n), (lax.rem(d + ND - 1, ND), 0, 2 * YS)]
        ):
            part = pl.ds(first_plane, planes)
            src = mod_h.at[part, pl.ds(at, n)] if a == 3 else u_h.at[a, part, pl.ds(at, n)]
            out.append(
                pltpu.make_async_remote_copy(
                    src, nat.at[a, pl.ds(HALO + first_plane, planes), pl.ds(to, n)],
                    usend.at[s, a], urecv.at[s, a], device_id=(g, k), device_id_type=MESH,
                )
            )
        return out

    def x_copies(a):
        out = []
        for s, (k, at, to) in enumerate(
            [(lax.rem(g + 1, NG), XS, 0), (lax.rem(g + NG - 1, NG), HALO, HALO + XS)]
        ):
            out.append(
                pltpu.make_async_remote_copy(
                    nat.at[a, pl.ds(at, HALO)], nat.at[a, pl.ds(to, HALO)],
                    xsend.at[s, a], xrecv.at[s, a], device_id=(k, d), device_id_type=MESH,
                )
            )
        return out

    order = [3, 0, 1, 2]
    pieces = [(a, j * XS // 4) for a in order for j in range(4)]

    def trickle(n):
        for _ in range(n):
            if pieces:
                a, at = pieces.pop(0)
                start_pair(y_copies(a, at, XS // 4), has_hi, has_lo)

    def pass_on(a):
        recv_pair(y_copies(a), has_hi, has_lo)
        start_pair(x_copies(a), has_east, has_west)

    def relay_copies(a):
        dst = gain if a == 3 else ua.at[a]
        return [
            pltpu.make_async_copy(
                nat.at[a, pl.ds(c * SL, SL)], dst.at[:, :, c], relay_sem.at[a, c]
            )
            for c in range(CH)
        ]

    def relay(a):
        recv_pair(x_copies(a), has_east, has_west)
        send_pair(x_copies(a), has_east, has_west)
        for c in relay_copies(a):
            c.start()

    pl.semaphore_wait(barrier, NF - 1)

    for j in range(PARTS):
        start_pair(halo_copies(0, j), to_after, to_before)

    @pl.when(to_after)
    def _():
        tx_copy.start()

    well_ids = [well_ref[b].astype(F32) for b in range(BLOCKS)]
    msg[0, 0:1] = block_sums(press[0])
    msg[1, 0:1] = lanes(weight_sums)
    msg[2, 0:1] = lanes([w + 1.0 for w in well_ids])
    join_copy(0).start()
    start_gather(0)

    p0 = press[0]
    storage = rdiag[...]
    base[...] = storage * p0 - BIOT * base[...]
    east[...] = jnp.where(last, 0.0, east[...])
    north[...] = jnp.where(iota((NY, NZ), 0) == NY - 1, 0.0, north[...])
    south[...] = prev_y(north[...])
    upper[...] = jnp.where(iota((NY, NZ), 1) == NZ - 1, 0.0, upper[...])
    lower[...] = pltpu.roll(upper[...], 1, 1)
    partial_sum = storage + east[...] + north[...] + south[...] + upper[...] + lower[...]
    for b in range(BLOCKS):
        partial_sum = partial_sum + wells[b]
    rdiag[...] = partial_sum
    own_u.wait()
    own_m.wait()

    def own_terms(p):
        acc = base[...] + north[...] * next_y(p) + south[...] * prev_y(p)
        return acc + upper[...] * pltpu.roll(p, NZ - 1, 1) + lower[...] * pltpu.roll(p, 1, 1)

    rates, strengths = [], []

    def find_wells():
        rate_at = iota((1, 256), 1).astype(F32)
        for n, (at_g, at_d) in enumerate([(g, d), before, after]):
            row = (at_g // 2) * ND + at_d
            first_lane = lax.rem(at_g, 2) * BLOCKS
            ids = ag0[2, pl.ds(row, 1), :]
            for b in range(BLOCKS):
                well = jnp.sum(jnp.where(lane == first_lane + b, ids, 0.0), axis=1, keepdims=True)
                mask = jnp.where(ag0[2] == well, 1.0, 0.0)
                masks[n * BLOCKS + b] = mask
                strengths.append(total(mask * ag0[1]))
                rates.append(
                    jnp.sum(
                        jnp.where(rate_at == well - 1.0, rate_ref[...], 0.0), axis=1, keepdims=True
                    )
                )

    def bottoms_of(k, count):
        sums = ag0[0] if k == 0 else ag[k - 1]
        return [(rates[n] + total(masks[n] * sums)) / strengths[n] for n in range(count)]

    for k in range(FLOW_SWEEPS + 1):
        if k == 0:
            field[...] = own_terms(p0)

            @pl.when(to_before)
            def _():
                tx_copy.wait_recv()

            rdiag[...] = 1.0 / (rdiag[...] + west[...])
            gather_wait(0, ag_recv.at[0])
            find_wells()
            bottoms = bottoms_of(0, BLOCKS)
            inflow = wells[0] * bottoms[0]
            for b in range(1, BLOCKS):
                inflow = inflow + wells[b] * bottoms[b]
            field[...] += inflow
        elif k == 1:
            p = press[1]
        else:
            gather_wait(k - 1, ag_recv.at[k - 1])
            bottoms = bottoms_of(k - 1, 3 * BLOCKS if k < FLOW_SWEEPS else BLOCKS)
            p = press[k]
            for b in range(BLOCKS):
                p = p + sinks[b] * bottoms[b]
        if k == FLOW_SWEEPS:
            ppad[YS : YS + NY, :] = p
            break
        if k > 0:
            msg[2 + k, 0:1] = block_sums(p)
            join_copy(k).start()
            field[...] = own_terms(p)
            start_gather(k)
        if k > 1:
            from_lo = near[0] * bottoms[BLOCKS]
            from_hi = near[BLOCKS] * bottoms[2 * BLOCKS]
            for b in range(1, BLOCKS):
                from_lo = from_lo + near[b] * bottoms[BLOCKS + b]
                from_hi = from_hi + near[BLOCKS + b] * bottoms[2 * BLOCKS + b]
            field[...] += east[...] * from_hi + west[...] * from_lo
        for j in range(PARTS):
            send_pair(halo_copies(k, j), to_after, to_before)
        trickle(4)
        for j in range(PARTS):
            part = slice(j * PR, (j + 1) * PR)
            recv_pair(halo_copies(k, j), to_after, to_before)
            acc = field[part] + east[part] * halo_hi[k, part] + west[part] * halo_lo[k, part]
            press[k + 1, part] = acc * rdiag[part]
            if k < FLOW_SWEEPS - 1:
                start_pair(halo_copies(k + 1, j), to_after, to_before)
        if k == 0:
            found = jnp.zeros((NY, BLOCKS * 128), F32)
            for third in thirds(rdiag[...]):
                found = found + jnp.dot(third, col_hot[...], preferred_element_type=F32)
            for b in range(BLOCKS):
                at_row = iota((NY, 128), 0) == cell_ref[b : b + 1, :] // NZ
                at_cell = jnp.where(at_row, found[:, b * 128 : (b + 1) * 128], 0.0)
                at_cell = jnp.sum(at_cell, axis=0, keepdims=True)
                near_msg[BLOCKS + b : BLOCKS + b + 1, :] = weights[b] * at_cell
                sinks[b] = wells[b] * rdiag[...]
            start_pair(near_copies, to_after, to_before)
        if k == 1:
            recv_pair(near_copies, to_after, to_before)
            for s, buffer in enumerate([near_lo, near_hi]):
                for b in range(BLOCKS):
                    near[s * BLOCKS + b] = dense(
                        buffer[b : b + 1, :].astype(jnp.int32), buffer[BLOCKS + b : BLOCKS + b + 1, :]
                    )
        if k > 0:
            pass_on(order[k - 1])

    def window(t):
        return ppad.at[pl.ds(pl.multiple_of(t * YS, YS), YW)]

    def place(x):
        return pwin.at[lax.rem(x, SL), :, x // SL]

    own_window = pltpu.make_async_copy(window(d), place(HALO + d), pw_self)
    own_window.start()

    def spread(first_step, x, target, j):
        def send(i, carry):
            t = lax.rem(d + i, ND)
            pltpu.make_async_remote_copy(
                window(t), place(x), pw_send.at[j], pw_recv.at[j],
                device_id=(target, t), device_id_type=MESH,
            ).start()
            return carry

        lax.fori_loop(first_step, ND, send, 0)

    spread(1, HALO + d, g, 0)
    to_hi = jnp.logical_and(d >= XS - HALO, has_east)
    to_lo = jnp.logical_and(d < HALO, has_west)

    @pl.when(to_hi)
    def _():
        spread(0, d - (XS - HALO), g + 1, 1)

    @pl.when(to_lo)
    def _():
        spread(0, HALO + XS + d, g - 1, 2)

    p_copy = pltpu.make_async_copy(ppad.at[pl.ds(YS, NY)], p_out.at[0], out_sem.at[0])
    p_copy.start()

    def window_wait(count, sem):
        part = nat.at[0, pl.ds(0, count)]
        pltpu.make_async_copy(part, part, sem).wait()

    relay(order[0])
    pass_on(order[3])
    for c in relay_copies(3):
        c.wait()

    def gain_row(y, carry):
        gy = (d - 1) * YS + y
        inside = jnp.logical_and(gy >= 0, gy < NY)
        scale = jnp.where(inside, -0.5 * BIOT / BETA * RELAX / 26.0, 0.0)
        for i in range(SL):
            gain[i, y] = scale * betas[i] / gain[i, y]
        return carry

    lax.fori_loop(2, YW - 2, gain_row, 0)
    for a in order[1:]:
        relay(a)
    for a in range(3):
        for c in relay_copies(a):
            c.wait()

    @pl.when(jnp.logical_not(last))
    def _():
        tx_copy.wait_send()

    for k in range(FLOW_SWEEPS):
        gather_wait(k, ag_send.at[k])
        join_copy(k).wait_send()
    send_pair(near_copies, to_after, to_before)
    for a in range(4):
        send_pair(y_copies(a), has_hi, has_lo)
    window_wait(ND - 1, pw_send.at[0])

    @pl.when(to_hi)
    def _():
        window_wait(ND, pw_send.at[1])

    @pl.when(to_lo)
    def _():
        window_wait(ND, pw_send.at[2])

    own_window.wait()
    window_wait(ND - 1, pw_recv.at[0])

    @pl.when(has_west)
    def _():
        window_wait(HALO, pw_recv.at[1])

    @pl.when(has_east)
    def _():
        window_wait(HALO, pw_recv.at[2])

    def force_row(y, carry):
        p = extend([pwin[i, y] for i in range(SL)])
        for i in range(SL):
            r = gain[i, y]
            force[0, i, y] = r * (p[i + 2] - p[i])
            force[1, i, y] = r * (pwin[i, y + 1] - pwin[i, y - 1])
            force[2, i, y] = r * (next_z(p[i + 1]) - prev_z(p[i + 1]))
        return carry

    lax.fori_loop(2, YW - 2, force_row, 0)

    def sweep_tools(s):
        src, dst = (ua, ub) if s % 2 == 0 else (ub, ua)

        def row_values(y, src=src):
            tz, dz = [], []
            for c in range(3):
                t, q = [], []
                for i in range(SL):
                    v = src[c, i, y]
                    hi, lo = next_z(v), prev_z(v)
                    t.append(v + hi + lo)
                    q.append(hi - lo)
                tz.append(extend(t))
                dz.append(q)
            sums = []
            for t in tz:
                r = []
                for i in range(0, SL, 2):
                    pair = t[i + 1] + t[i + 2]
                    r += [t[i] + pair, pair + t[i + 3]]
                sums.append(r)
            ux = extend([src[0, i, y] for i in range(SL)])
            dx = extend(dz[0])
            along_y = [ux[i + 2] - ux[i] + dz[2][i] for i in range(SL)]
            cross = [dx[i + 2] - dx[i] for i in range(SL)]
            return sums, along_y, dz[1], dz[2], cross

        def row_store(y, values):
            sums, along_y, dzy, dzz, cross = values
            for i in range(SL):
                for c in range(3):
                    xsum[c, i, y] = sums[c][i]
                shear[i, y] = along_y[i]
                dy_z[i, y] = dzy[i]
                dz_z[i, y] = dzz[i]
                dx_z[i, y] = cross[i]

        def combine(y, src=src, dst=dst):
            gy = (d - 1) * YS + y
            inside = jnp.logical_and(gy >= 0, gy < NY).astype(F32)
            along_x = extend([src[1, i, y + 1] - src[1, i, y - 1] + dz_z[i, y] for i in range(SL)])
            for i in range(SL):
                beta = betas[i] * inside
                mixed = [
                    along_x[i + 2] - along_x[i],
                    shear[i, y + 1] - shear[i, y - 1],
                    dx_z[i, y] + dy_z[i, y + 1] - dy_z[i, y - 1],
                ]
                for c in range(3):
                    box = xsum[c, i, y - 1] + xsum[c, i, y] + xsum[c, i, y + 1]
                    r = box + COUPLE * mixed[c] + (ALPHA / BETA) * src[c, i, y]
                    dst[c, i, y] = beta * r + force[c, i, y]

        return row_values, row_store, combine

    def first_rows(s, row_values):
        return [(y, row_values(y)) for y in (1 + s, 2 + s, 3 + s)]

    tools = [sweep_tools(s) for s in range(MECH_SWEEPS)]
    for y, values in first_rows(0, tools[0][0]):
        tools[0][1](y, values)
    for s, (row_values, row_store, combine) in enumerate(tools):
        y0, y1 = 2 + s, YW - 2 - s

        def mech_row(y, carry, row_values=row_values, row_store=row_store, combine=combine):
            values = row_values(y + 2)
            combine(y)
            row_store(y + 2, values)
            return carry

        lax.fori_loop(y0, y1 - 2, mech_row, 0, unroll=2)
        values = row_values(y1)
        combine(y1 - 2)
        row_store(y1, values)
        ahead = first_rows(s + 1, tools[s + 1][0]) if s < MECH_SWEEPS - 1 else []
        combine(y1 - 1)
        for y, values in ahead:
            row_store(y, values)

    final = ua if MECH_SWEEPS % 2 == 0 else ub

    def strain_row(y, carry):
        ux = extend([final[0, i, y] for i in range(SL)])
        for i in range(SL):
            uz = final[2, i, y]
            div = ux[i + 2] - ux[i] + final[1, i, y + 1] - final[1, i, y - 1]
            strain[i, y - YS] = 0.5 * (div + next_z(uz) - prev_z(uz))
        return carry

    lax.fori_loop(YS, 2 * YS, strain_row, 0)
    rows = pl.ds(pl.multiple_of(d * YS, YS), YS)

    def strain_of(t):
        x = t + HALO
        return strain.at[lax.rem(x, SL), :, x // SL]

    def send_strain(i, carry):
        t = lax.rem(d + i, ND)
        pltpu.make_async_remote_copy(
            strain_of(t), s_out.at[0, rows], st_send, st_recv,
            device_id=(g, t), device_id_type=MESH,
        ).start()
        return carry

    lax.fori_loop(1, ND, send_strain, 0)
    own_strain = pltpu.make_async_copy(strain_of(d), s_out.at[0, rows], st_self)
    own_strain.start()
    u_copies = []
    for c in range(CH):
        lo, hi = max(c * SL, HALO), min((c + 1) * SL, HALO + XS)
        if lo < hi:
            u_copies.append(
                pltpu.make_async_copy(
                    final.at[:, pl.ds(lo - c * SL, hi - lo), pl.ds(YS, YS), c],
                    u_out.at[:, pl.ds(lo - HALO, hi - lo)],
                    out_sem.at[1 + c],
                )
            )
    for c in u_copies:
        c.start()

    p_copy.wait()
    for c in u_copies:
        c.wait()
    own_strain.wait()
    part = ppad.at[pl.ds(0, (ND - 1) * YS)]
    pltpu.make_async_copy(part, part, st_send).wait()
    pltpu.make_async_copy(part, part, st_recv).wait()


def hand_over(p_in, u_in, s_in, p_out, u_out, s_out, p_buf, u_buf, s_buf, sem_in, sem_out):
    pairs = []
    half = NY // 2
    for src, buf, dst in [(p_in, p_buf, p_out), (s_in, s_buf, s_out)]:
        for j in range(2):
            part = pl.ds(j * half, half)
            pairs.append((src.at[0, part], buf.at[0, part], dst.at[0, part]))
    for c in range(3):
        for j in range(2):
            part = pl.ds(j * XS // 2, XS // 2)
            pairs.append((u_in.at[c, part], u_buf.at[c, part], u_out.at[c, part]))
    loads = [pltpu.make_async_copy(a, b, sem_in.at[i]) for i, (a, b, _) in enumerate(pairs)]
    saves = [pltpu.make_async_copy(b, c, sem_out.at[i]) for i, (_, b, c) in enumerate(pairs)]
    for c in loads:
        c.start()
    for c, s in zip(loads, saves):
        c.wait()
        s.start()
    for s in saves:
        s.wait()


def body(
    pressure_old, strain_change, storage, trans_x, trans_y, trans_z, displacement_old, modulus,
    perf_cell, perf_well, perf_count, perf_index, well_rate,
):
    dma = pltpu.SemaphoreType.DMA
    vmem = lambda *shape: pltpu.VMEM(shape, F32)
    plane = (NY, NZ)
    slabs = (SL, YW, CH, NZ)
    hbm = pl.BlockSpec(memory_space=pl.ANY)
    shapes = (
        jax.ShapeDtypeStruct((1, NY, NZ), F32),
        jax.ShapeDtypeStruct((3, XS, YS, NZ), F32),
        jax.ShapeDtypeStruct((1, NY, NZ), F32),
    )
    results = pl.pallas_call(
        kernel,
        name="poro_step",
        out_shape=shapes,
        in_specs=[hbm] * 13,
        out_specs=(hbm, hbm, hbm),
        scratch_shapes=[
            pltpu.VMEM((BLOCKS, 128), jnp.int32),
            pltpu.SMEM((BLOCKS,), jnp.int32),
            pltpu.SMEM((BLOCKS,), jnp.int32),
            vmem(BLOCKS, 128),
            vmem(1, 256),
            vmem(FLOW_SWEEPS + 1, *plane),
            vmem(*plane),
            vmem(*plane),
            vmem(*plane),
            vmem(*plane),
            vmem(*plane),
            vmem(*plane),
            vmem(*plane),
            vmem(*plane),
            vmem(*plane),
            vmem(BLOCKS, *plane),
            vmem(BLOCKS, *plane),
            vmem(2 * BLOCKS, *plane),
            vmem(FLOW_SWEEPS, *plane),
            vmem(FLOW_SWEEPS, *plane),
            pltpu.VMEM((NZ, BLOCKS * 128), jnp.bfloat16),
            vmem(2 * BLOCKS, 128),
            vmem(2 * BLOCKS, 128),
            vmem(2 * BLOCKS, 128),
            vmem(3 + FLOW_SWEEPS - 1, 8, 128),
            vmem(3 + FLOW_SWEEPS - 1, 8, 128),
            vmem(3 + FLOW_SWEEPS - 1, 8, 128),
            vmem(3, CHIPS, 128),
            vmem(FLOW_SWEEPS - 1, CHIPS, 128),
            vmem(3 * BLOCKS, CHIPS, 128),
            vmem(NY + 2 * YS, NZ),
            vmem(4, XW, YW, NZ),
            vmem(*slabs),
            vmem(3, *slabs),
            vmem(3, *slabs),
            vmem(*slabs),
            vmem(3, *slabs),
            vmem(3, *slabs),
            vmem(*slabs),
            vmem(*slabs),
            vmem(*slabs),
            vmem(*slabs),
            vmem(SL, CH, NZ),
            vmem(SL, YS, CH, NZ),
            dma((5,)),
            dma((6,)),
            dma((2,)),
            dma((2, FLOW_SWEEPS, PARTS)),
            dma((2, FLOW_SWEEPS, PARTS)),
            dma,
            dma,
            dma((2,)),
            dma((2,)),
            dma((FLOW_SWEEPS,)),
            dma((FLOW_SWEEPS,)),
            dma((FLOW_SWEEPS,)),
            dma((FLOW_SWEEPS,)),
            dma((2, 4)),
            dma((2, 4)),
            dma((2, 4)),
            dma((2, 4)),
            dma((4, CH)),
            dma((3,)),
            dma((3,)),
            dma,
            dma,
            dma,
            dma,
            dma((1 + CH,)),
        ],
        compiler_params=pltpu.CompilerParams(
            collective_id=0, has_side_effects=True, vmem_limit_bytes=62 << 20
        ),
    )(
        pressure_old, strain_change, storage, trans_x, trans_y, trans_z, displacement_old, modulus,
        perf_cell, perf_well, perf_count, perf_index,
        well_rate.reshape(1, -1),
    )
    return pl.pallas_call(
        hand_over,
        name="hand_over",
        out_shape=shapes,
        in_specs=[hbm] * 3,
        out_specs=(hbm, hbm, hbm),
        scratch_shapes=[
            vmem(1, NY, NZ),
            vmem(3, XS, YS, NZ),
            vmem(1, NY, NZ),
            dma((10,)),
            dma((10,)),
        ],
    )(*results)


def solution(mesh):
    flow = P(("grp", "dev"), None, None)
    slabs = P(None, "grp", "dev", None)
    return jax.shard_map(
        body,
        mesh=mesh,
        in_specs=(
            flow, flow, flow, flow, flow, flow, slabs, P("grp", "dev", None),
            P(("grp", "dev"), None), P(("grp", "dev")), P(("grp", "dev")), P(("grp", "dev"), None), P(),
        ),
        out_specs=(flow, slabs, flow),
        check_vma=False,
    )
```

```python
import functools

import jax
import jax.numpy as jnp
from jax import lax
from jax.experimental import pallas as pl
from jax.experimental.pallas import tpu as pltpu
from jax.sharding import PartitionSpec as P

MESH = pl.DeviceIdType.MESH
F32 = jnp.float32

FLOW_SWEEPS = 4
MECH_SWEEPS = 6
BIOT = 0.8
RELAX = 0.6
COUPLE = 0.375

NG, ND = 4, 32
NF = NG * ND
CHIPS = NF // 2
NY, NZ = 256, 256
XS, YS = 32, 8
HALO = MECH_SWEEPS + 1
CH, SL = 8, 6
XW = CH * SL
YW = 3 * YS
BLOCKS = 4
PARTS = 2
PR = NY // PARTS

ALPHA = 1.0 - RELAX * 27.0 / 26.0
BETA = RELAX / 26.0


def iota(shape, dim):
    return lax.broadcasted_iota(jnp.int32, shape, dim)


def next_z(v):
    n = v.shape[-1]
    return jnp.where(iota(v.shape, 1) == n - 1, 0.0, pltpu.roll(v, n - 1, 1))


def prev_z(v):
    return jnp.where(iota(v.shape, 1) == 0, 0.0, pltpu.roll(v, 1, 1))


def next_y(v):
    return pltpu.roll(v, v.shape[0] - 1, 0)


def prev_y(v):
    return pltpu.roll(v, 1, 0)


def extend(slots):
    return [pltpu.roll(slots[-1], 1, 0)] + slots + [pltpu.roll(slots[0], CH - 1, 0)]


def total(v):
    return jnp.sum(jnp.sum(v, axis=0, keepdims=True), axis=1, keepdims=True)


def kernel(
    p0_h, sc_h, st_h, tx_h, ty_h, tz_h, u_h, mod_h, cell_h, well_h, cnt_h, idx_h, rate_h,
    p_out, u_out, s_out,
    cell_ref, well_ref, cnt_ref, idx_ref, rate_ref,
    press, field, base, east, west, north, south, upper, lower, rdiag, wells, sinks, near,
    halo_lo, halo_hi, col_hot, near_msg, near_lo, near_hi, msg, other, joint, ag0, ag, masks,
    ppad, nat, pwin, ua, ub, gain, force, xsum, shear, dy_z, dz_z, dx_z, betas, strain,
    small_sem, load_sem, uload_sem, halo_send, halo_recv, tx_send, tx_recv, near_send, near_recv, join_send, join_recv, ag_send, ag_recv,
    usend, urecv, xsend, xrecv, relay_sem, pw_send, pw_recv, pw_self, st_send, st_recv, st_self,
    out_sem,
):
    g = lax.axis_index("grp")
    d = lax.axis_index("dev")
    f = g * ND + d
    first, last = f == 0, f == NF - 1
    has_lo, has_hi = d > 0, d < ND - 1
    has_west, has_east = g > 0, g < NG - 1

    def flow_dev(k):
        return (k // ND, lax.rem(k, ND))

    after, before = flow_dev(lax.rem(f + 1, NF)), flow_dev(lax.rem(f + NF - 1, NF))

    small_loads = [
        pltpu.make_async_copy(src, dst, small_sem.at[i])
        for i, (src, dst) in enumerate(
            [
                (cell_h, cell_ref),
                (well_h, well_ref),
                (cnt_h, cnt_ref),
                (idx_h, idx_ref),
                (rate_h, rate_ref),
            ]
        )
    ]
    plane_loads = [
        pltpu.make_async_copy(src.at[0], dst, load_sem.at[i])
        for i, (src, dst) in enumerate(
            [
                (p0_h, press.at[0]),
                (sc_h, base),
                (st_h, rdiag),
                (tx_h, east),
                (ty_h, north),
                (tz_h, upper),
            ]
        )
    ]
    own_u = pltpu.make_async_copy(
        u_h, nat.at[pl.ds(0, 3), pl.ds(HALO, XS), pl.ds(YS, YS)], uload_sem.at[0]
    )
    own_m = pltpu.make_async_copy(
        mod_h, nat.at[3, pl.ds(HALO, XS), pl.ds(YS, YS)], uload_sem.at[1]
    )
    for c in small_loads + plane_loads + [own_u, own_m]:
        c.start()

    def fill(planes, rows):
        n, m = planes.stop - planes.start, rows.stop - rows.start
        nat[0:3, planes, rows, :] = jnp.zeros((3, n, m, NZ), F32)
        nat[3, planes, rows, :] = jnp.ones((n, m, NZ), F32)

    own_planes, all_rows = slice(HALO, HALO + XS), slice(0, YW)
    fill(slice(2 * HALO + XS, XW), all_rows)
    pwin[...] = jnp.zeros(pwin.shape, F32)

    @pl.when(d == 0)
    def _():
        fill(own_planes, slice(0, YS))

    @pl.when(d == ND - 1)
    def _():
        fill(own_planes, slice(2 * YS, YW))

    @pl.when(g == 0)
    def _():
        fill(slice(0, HALO), all_rows)

    @pl.when(g == NG - 1)
    def _():
        fill(slice(HALO + XS, 2 * HALO + XS), all_rows)

    barrier = pltpu.get_barrier_semaphore()

    core, z_lo = lax.rem(g, 2), g // 2
    z_hi, phys_x, phys_y = d // 16, lax.rem(d // 4, 4), lax.rem(d, 4)
    phys_z = 2 * z_hi + z_lo
    spots = sorted(
        ((x, y) for x in range(4) for y in range(4)),
        key=lambda o: -(min(o[0], 4 - o[0]) + min(o[1], 4 - o[1])),
    )
    for ox, oy in spots:
        x, y = lax.rem(phys_x + ox, 4), lax.rem(phys_y + oy, 4)

        def greet(j, carry, x=x, y=y):
            z = lax.rem(phys_z + lax.rem(2 + 3 * (j // 2), 4), 4)
            c = lax.rem(core + 1 + lax.rem(j, 2), 2)
            pl.semaphore_signal(
                barrier, inc=1, device_id=(lax.rem(z, 2) * 2 + c, (z // 2) * 16 + x * 4 + y),
                device_id_type=MESH,
            )
            return carry

        if ox == 0 and oy == 0:
            lax.fori_loop(0, 5, greet, 0)
            lax.fori_loop(6, 8, greet, 0)
        else:
            lax.fori_loop(0, 8, greet, 0)

    @pl.when(first)
    def _():
        halo_lo[...] = jnp.zeros(halo_lo.shape, F32)
        near_lo[...] = jnp.zeros(near_lo.shape, F32)
        west[...] = jnp.zeros((NY, NZ), F32)

    @pl.when(last)
    def _():
        halo_hi[...] = jnp.zeros(halo_hi.shape, F32)
        near_hi[...] = jnp.zeros(near_hi.shape, F32)

    ppad[0:YS, :] = jnp.zeros((YS, NZ), F32)
    ppad[NY + YS :, :] = jnp.zeros((YS, NZ), F32)
    for i in range(SL):
        x = iota((CH, NZ), 0) * SL + i + g * XS - HALO
        betas[i] = jnp.where(jnp.logical_and(x >= 0, x < NG * XS), BETA, 0.0)

    for c in small_loads:
        c.wait()
    lane = iota((1, 128), 1)

    def hot(shape, index):
        return jnp.where(iota(shape, 0) == index, 1.0, 0.0).astype(jnp.bfloat16)

    def thirds(v):
        out = []
        for _ in range(3):
            part = v.astype(jnp.bfloat16)
            v = v - part.astype(F32)
            out.append(part)
        return out

    def dense(cell, value):
        at_row = iota((NY, 128), 0) == cell // NZ
        at_col = hot((NZ, 128), lax.rem(cell, NZ))
        plane = jnp.zeros((NY, NZ), F32)
        for part in thirds(value):
            spread = jnp.where(at_row, part.astype(F32), 0.0).astype(jnp.bfloat16)
            plane = plane + lax.dot_general(
                spread, at_col, (((1,), (1,)), ((), ())), preferred_element_type=F32
            )
        return plane

    weights = []
    for b in range(BLOCKS):
        weight = jnp.where(lane < cnt_ref[b], idx_ref[b : b + 1, :], 0.0)
        cell = cell_ref[b : b + 1, :]
        wells[b] = dense(cell, weight)
        col_hot[:, b * 128 : (b + 1) * 128] = hot((NZ, 128), lax.rem(cell, NZ))
        near_msg[b : b + 1, :] = cell.astype(F32)
        weights.append(weight)
    weight_sums = [jnp.sum(w, axis=1, keepdims=True) for w in weights]

    for c in plane_loads:
        c.wait()

    def start_pair(copies, to_up, to_down):
        @pl.when(to_up)
        def _():
            copies[0].start()

        @pl.when(to_down)
        def _():
            copies[1].start()

    def recv_pair(copies, to_up, to_down):
        @pl.when(to_down)
        def _():
            copies[0].wait_recv()

        @pl.when(to_up)
        def _():
            copies[1].wait_recv()

    def send_pair(copies, to_up, to_down):
        @pl.when(to_up)
        def _():
            copies[0].wait_send()

        @pl.when(to_down)
        def _():
            copies[1].wait_send()

    def halo_copies(k, j):
        part = pl.ds(j * PR, PR)
        return [
            pltpu.make_async_remote_copy(
                press.at[k, part], buffer.at[k, part], halo_send.at[s, k, j], halo_recv.at[s, k, j],
                device_id=target, device_id_type=MESH,
            )
            for s, (buffer, target) in enumerate([(halo_lo, after), (halo_hi, before)])
        ]

    tx_copy = pltpu.make_async_remote_copy(
        tx_h.at[0], west, tx_send, tx_recv, device_id=after, device_id_type=MESH
    )
    near_copies = [
        pltpu.make_async_remote_copy(
            near_msg, buffer, near_send.at[s], near_recv.at[s], device_id=target, device_id_type=MESH
        )
        for s, (buffer, target) in enumerate([(near_lo, after), (near_hi, before)])
    ]
    to_after, to_before = jnp.logical_not(last), jnp.logical_not(first)

    chip = z_lo * ND + d

    def lanes(values):
        out = jnp.zeros((1, 128), F32)
        for b, v in enumerate(values):
            out = jnp.where(lane == core * BLOCKS + b, v, out)
        return out

    def block_sums(p):
        return lanes([total(wells[b] * p) for b in range(BLOCKS)])

    def rows_of(ref, k):
        return ref.at[pl.ds(0, 3), pl.ds(0, 1)] if k == 0 else ref.at[2 + k, pl.ds(0, 1)]

    def gathered(k, r, n):
        return ag0.at[:, pl.ds(r, n)] if k == 0 else ag.at[k - 1, pl.ds(r, n)]

    def join_copy(k):
        return pltpu.make_async_remote_copy(
            rows_of(msg, k), rows_of(other, k), join_send.at[k], join_recv.at[k],
            device_id=(z_lo * 2 + 1 - core, d), device_id_type=MESH,
        )

    def start_gather(k):
        join_copy(k).wait_recv()
        for j in range(3) if k == 0 else [2 + k]:
            row = msg[j, 0:1] + other[j, 0:1]
            joint[j, 0:1] = row
            if k == 0:
                ag0[j, pl.ds(chip, 1), :] = row
            else:
                ag[k - 1, pl.ds(chip, 1), :] = row

        def send(x, y, oz):
            z = lax.rem(phys_z + oz, 4)
            pltpu.make_async_remote_copy(
                rows_of(joint, k), gathered(k, chip, 1), ag_send.at[k], ag_recv.at[k],
                device_id=(lax.rem(z, 2) * 2 + core, (z // 2) * 16 + x * 4 + y), device_id_type=MESH,
            ).start()

        for ox, oy in spots:
            x, y = lax.rem(phys_x + ox, 4), lax.rem(phys_y + oy, 4)
            if ox == 0 and oy == 0:
                for oz in (2, 1, 3):
                    send(x, y, oz)
            else:

                def step(j, carry, x=x, y=y):
                    send(x, y, lax.rem(2 + 3 * j, 4))
                    return carry

                lax.fori_loop(0, 4, step, 0)

    def gather_wait(k, sem):
        part = gathered(k, 0, CHIPS - 1)
        pltpu.make_async_copy(part, part, sem).wait()

    def y_copies(a, first_plane=0, planes=XS):
        n = HALO - 1 if a == 3 else HALO
        out = []
        for s, (k, at, to) in enumerate(
            [(lax.rem(d + 1, ND), YS - n, YS - n), (lax.rem(d + ND - 1, ND), 0, 2 * YS)]
        ):
            part = pl.ds(first_plane, planes)
            src = mod_h.at[part, pl.ds(at, n)] if a == 3 else u_h.at[a, part, pl.ds(at, n)]
            out.append(
                pltpu.make_async_remote_copy(
                    src, nat.at[a, pl.ds(HALO + first_plane, planes), pl.ds(to, n)],
                    usend.at[s, a], urecv.at[s, a], device_id=(g, k), device_id_type=MESH,
                )
            )
        return out

    def x_copies(a):
        out = []
        for s, (k, at, to) in enumerate(
            [(lax.rem(g + 1, NG), XS, 0), (lax.rem(g + NG - 1, NG), HALO, HALO + XS)]
        ):
            out.append(
                pltpu.make_async_remote_copy(
                    nat.at[a, pl.ds(at, HALO)], nat.at[a, pl.ds(to, HALO)],
                    xsend.at[s, a], xrecv.at[s, a], device_id=(k, d), device_id_type=MESH,
                )
            )
        return out

    order = [3, 0, 1, 2]
    pieces = [(a, j * XS // 4) for a in order for j in range(4)]

    def trickle(n):
        for _ in range(n):
            if pieces:
                a, at = pieces.pop(0)
                start_pair(y_copies(a, at, XS // 4), has_hi, has_lo)

    def pass_on(a):
        recv_pair(y_copies(a), has_hi, has_lo)
        start_pair(x_copies(a), has_east, has_west)

    def relay_copies(a):
        dst = gain if a == 3 else ua.at[a]
        return [
            pltpu.make_async_copy(
                nat.at[a, pl.ds(c * SL, SL)], dst.at[:, :, c], relay_sem.at[a, c]
            )
            for c in range(CH)
        ]

    def relay(a):
        recv_pair(x_copies(a), has_east, has_west)
        send_pair(x_copies(a), has_east, has_west)
        for c in relay_copies(a):
            c.start()

    pl.semaphore_wait(barrier, NF - 1)

    for j in range(PARTS):
        start_pair(halo_copies(0, j), to_after, to_before)

    @pl.when(to_after)
    def _():
        tx_copy.start()

    well_ids = [well_ref[b].astype(F32) for b in range(BLOCKS)]
    msg[0, 0:1] = block_sums(press[0])
    msg[1, 0:1] = lanes(weight_sums)
    msg[2, 0:1] = lanes([w + 1.0 for w in well_ids])
    join_copy(0).start()
    start_gather(0)

    p0 = press[0]
    storage = rdiag[...]
    base[...] = storage * p0 - BIOT * base[...]
    east[...] = jnp.where(last, 0.0, east[...])
    north[...] = jnp.where(iota((NY, NZ), 0) == NY - 1, 0.0, north[...])
    south[...] = prev_y(north[...])
    upper[...] = jnp.where(iota((NY, NZ), 1) == NZ - 1, 0.0, upper[...])
    lower[...] = pltpu.roll(upper[...], 1, 1)
    partial_sum = storage + east[...] + north[...] + south[...] + upper[...] + lower[...]
    for b in range(BLOCKS):
        partial_sum = partial_sum + wells[b]
    rdiag[...] = partial_sum
    own_u.wait()
    own_m.wait()

    def own_terms(p):
        acc = base[...] + north[...] * next_y(p) + south[...] * prev_y(p)
        return acc + upper[...] * pltpu.roll(p, NZ - 1, 1) + lower[...] * pltpu.roll(p, 1, 1)

    rates, strengths = [], []

    def find_wells():
        rate_at = iota((1, 256), 1).astype(F32)
        for n, (at_g, at_d) in enumerate([(g, d), before, after]):
            row = (at_g // 2) * ND + at_d
            first_lane = lax.rem(at_g, 2) * BLOCKS
            ids = ag0[2, pl.ds(row, 1), :]
            for b in range(BLOCKS):
                well = jnp.sum(jnp.where(lane == first_lane + b, ids, 0.0), axis=1, keepdims=True)
                mask = jnp.where(ag0[2] == well, 1.0, 0.0)
                masks[n * BLOCKS + b] = mask
                strengths.append(total(mask * ag0[1]))
                rates.append(
                    jnp.sum(
                        jnp.where(rate_at == well - 1.0, rate_ref[...], 0.0), axis=1, keepdims=True
                    )
                )

    def bottoms_of(k, count):
        sums = ag0[0] if k == 0 else ag[k - 1]
        return [(rates[n] + total(masks[n] * sums)) / strengths[n] for n in range(count)]

    for k in range(FLOW_SWEEPS + 1):
        if k == 0:
            field[...] = own_terms(p0)

            @pl.when(to_before)
            def _():
                tx_copy.wait_recv()

            rdiag[...] = 1.0 / (rdiag[...] + west[...])
            gather_wait(0, ag_recv.at[0])
            find_wells()
            bottoms = bottoms_of(0, BLOCKS)
            inflow = wells[0] * bottoms[0]
            for b in range(1, BLOCKS):
                inflow = inflow + wells[b] * bottoms[b]
            field[...] += inflow
        elif k == 1:
            p = press[1]
        else:
            gather_wait(k - 1, ag_recv.at[k - 1])
            bottoms = bottoms_of(k - 1, 3 * BLOCKS if k < FLOW_SWEEPS else BLOCKS)
            p = press[k]
            for b in range(BLOCKS):
                p = p + sinks[b] * bottoms[b]
        if k == FLOW_SWEEPS:
            ppad[YS : YS + NY, :] = p
            break
        if k > 0:
            msg[2 + k, 0:1] = block_sums(p)
            join_copy(k).start()
            field[...] = own_terms(p)
            start_gather(k)
        if k > 1:
            from_lo = near[0] * bottoms[BLOCKS]
            from_hi = near[BLOCKS] * bottoms[2 * BLOCKS]
            for b in range(1, BLOCKS):
                from_lo = from_lo + near[b] * bottoms[BLOCKS + b]
                from_hi = from_hi + near[BLOCKS + b] * bottoms[2 * BLOCKS + b]
            field[...] += east[...] * from_hi + west[...] * from_lo
        for j in range(PARTS):
            send_pair(halo_copies(k, j), to_after, to_before)
        trickle([0, 4, 4, 4][k])
        for j in range(PARTS):
            part = slice(j * PR, (j + 1) * PR)
            recv_pair(halo_copies(k, j), to_after, to_before)
            acc = field[part] + east[part] * halo_hi[k, part] + west[part] * halo_lo[k, part]
            press[k + 1, part] = acc * rdiag[part]
            if k < FLOW_SWEEPS - 1:
                start_pair(halo_copies(k + 1, j), to_after, to_before)
        if k == 0:
            found = jnp.zeros((NY, BLOCKS * 128), F32)
            for third in thirds(rdiag[...]):
                found = found + jnp.dot(third, col_hot[...], preferred_element_type=F32)
            for b in range(BLOCKS):
                at_row = iota((NY, 128), 0) == cell_ref[b : b + 1, :] // NZ
                at_cell = jnp.where(at_row, found[:, b * 128 : (b + 1) * 128], 0.0)
                at_cell = jnp.sum(at_cell, axis=0, keepdims=True)
                near_msg[BLOCKS + b : BLOCKS + b + 1, :] = weights[b] * at_cell
                sinks[b] = wells[b] * rdiag[...]
            start_pair(near_copies, to_after, to_before)
        if k == 1:
            recv_pair(near_copies, to_after, to_before)
            for s, buffer in enumerate([near_lo, near_hi]):
                for b in range(BLOCKS):
                    near[s * BLOCKS + b] = dense(
                        buffer[b : b + 1, :].astype(jnp.int32), buffer[BLOCKS + b : BLOCKS + b + 1, :]
                    )

    def window(t):
        return ppad.at[pl.ds(pl.multiple_of(t * YS, YS), YW)]

    def place(x):
        return pwin.at[lax.rem(x, SL), :, x // SL]

    own_window = pltpu.make_async_copy(window(d), place(HALO + d), pw_self)
    own_window.start()

    def spread(first_step, x, target, j):
        def send(i, carry):
            t = lax.rem(d + i, ND)
            pltpu.make_async_remote_copy(
                window(t), place(x), pw_send.at[j], pw_recv.at[j],
                device_id=(target, t), device_id_type=MESH,
            ).start()
            return carry

        lax.fori_loop(first_step, ND, send, 0)

    spread(1, HALO + d, g, 0)
    to_hi = jnp.logical_and(d >= XS - HALO, has_east)
    to_lo = jnp.logical_and(d < HALO, has_west)

    @pl.when(to_hi)
    def _():
        spread(0, d - (XS - HALO), g + 1, 1)

    @pl.when(to_lo)
    def _():
        spread(0, HALO + XS + d, g - 1, 2)

    p_copy = pltpu.make_async_copy(ppad.at[pl.ds(YS, NY)], p_out.at[0], out_sem.at[0])
    p_copy.start()
    trickle(16)

    def window_wait(count, sem):
        part = nat.at[0, pl.ds(0, count)]
        pltpu.make_async_copy(part, part, sem).wait()

    pass_on(order[0])
    pass_on(order[1])
    pass_on(order[2])
    relay(order[0])
    relay(order[1])
    for c in relay_copies(3):
        c.wait()

    def gain_row(y, carry):
        gy = (d - 1) * YS + y
        inside = jnp.logical_and(gy >= 0, gy < NY)
        scale = jnp.where(inside, -0.5 * BIOT / BETA * RELAX / 26.0, 0.0)
        for i in range(SL):
            gain[i, y] = scale * betas[i] / gain[i, y]
        return carry

    lax.fori_loop(2, YW - 2, gain_row, 0)
    pass_on(order[3])
    relay(order[2])
    relay(order[3])
    for a in range(3):
        for c in relay_copies(a):
            c.wait()

    @pl.when(jnp.logical_not(last))
    def _():
        tx_copy.wait_send()

    for k in range(FLOW_SWEEPS):
        gather_wait(k, ag_send.at[k])
        join_copy(k).wait_send()
    send_pair(near_copies, to_after, to_before)
    for a in range(4):
        send_pair(y_copies(a), has_hi, has_lo)
    window_wait(ND - 1, pw_send.at[0])

    @pl.when(to_hi)
    def _():
        window_wait(ND, pw_send.at[1])

    @pl.when(to_lo)
    def _():
        window_wait(ND, pw_send.at[2])

    own_window.wait()
    window_wait(ND - 1, pw_recv.at[0])

    @pl.when(has_west)
    def _():
        window_wait(HALO, pw_recv.at[1])

    @pl.when(has_east)
    def _():
        window_wait(HALO, pw_recv.at[2])

    def force_row(y, carry):
        p = extend([pwin[i, y] for i in range(SL)])
        for i in range(SL):
            r = gain[i, y]
            force[0, i, y] = r * (p[i + 2] - p[i])
            force[1, i, y] = r * (pwin[i, y + 1] - pwin[i, y - 1])
            force[2, i, y] = r * (next_z(p[i + 1]) - prev_z(p[i + 1]))
        return carry

    lax.fori_loop(2, YW - 2, force_row, 0)

    def sweep_tools(s):
        src, dst = (ua, ub) if s % 2 == 0 else (ub, ua)

        def row_values(y, src=src):
            tz, dz = [], []
            for c in range(3):
                t, q = [], []
                for i in range(SL):
                    v = src[c, i, y]
                    hi, lo = next_z(v), prev_z(v)
                    t.append(v + hi + lo)
                    q.append(hi - lo)
                tz.append(extend(t))
                dz.append(q)
            sums = []
            for t in tz:
                r = []
                for i in range(0, SL, 2):
                    pair = t[i + 1] + t[i + 2]
                    r += [t[i] + pair, pair + t[i + 3]]
                sums.append(r)
            ux = extend([src[0, i, y] for i in range(SL)])
            dx = extend(dz[0])
            along_y = [ux[i + 2] - ux[i] + dz[2][i] for i in range(SL)]
            cross = [dx[i + 2] - dx[i] for i in range(SL)]
            return sums, along_y, dz[1], dz[2], cross

        def row_store(y, values):
            sums, along_y, dzy, dzz, cross = values
            for i in range(SL):
                for c in range(3):
                    xsum[c, i, y] = sums[c][i]
                shear[i, y] = along_y[i]
                dy_z[i, y] = dzy[i]
                dz_z[i, y] = dzz[i]
                dx_z[i, y] = cross[i]

        def combine(y, src=src, dst=dst):
            gy = (d - 1) * YS + y
            inside = jnp.logical_and(gy >= 0, gy < NY).astype(F32)
            along_x = extend([src[1, i, y + 1] - src[1, i, y - 1] + dz_z[i, y] for i in range(SL)])
            for i in range(SL):
                beta = betas[i] * inside
                mixed = [
                    along_x[i + 2] - along_x[i],
                    shear[i, y + 1] - shear[i, y - 1],
                    dx_z[i, y] + dy_z[i, y + 1] - dy_z[i, y - 1],
                ]
                for c in range(3):
                    box = xsum[c, i, y - 1] + xsum[c, i, y] + xsum[c, i, y + 1]
                    r = box + COUPLE * mixed[c] + (ALPHA / BETA) * src[c, i, y]
                    dst[c, i, y] = beta * r + force[c, i, y]

        return row_values, row_store, combine

    def first_rows(s, row_values):
        return [(y, row_values(y)) for y in (1 + s, 2 + s, 3 + s)]

    tools = [sweep_tools(s) for s in range(MECH_SWEEPS)]
    for y, values in first_rows(0, tools[0][0]):
        tools[0][1](y, values)
    for s, (row_values, row_store, combine) in enumerate(tools):
        y0, y1 = 2 + s, YW - 2 - s

        def mech_row(y, carry, row_values=row_values, row_store=row_store, combine=combine):
            values = row_values(y + 2)
            combine(y)
            row_store(y + 2, values)
            return carry

        lax.fori_loop(y0, y1 - 2, mech_row, 0, unroll=2)
        values = row_values(y1)
        combine(y1 - 2)
        row_store(y1, values)
        ahead = first_rows(s + 1, tools[s + 1][0]) if s < MECH_SWEEPS - 1 else []
        combine(y1 - 1)
        for y, values in ahead:
            row_store(y, values)

    final = ua if MECH_SWEEPS % 2 == 0 else ub

    def strain_row(y, carry):
        ux = extend([final[0, i, y] for i in range(SL)])
        for i in range(SL):
            uz = final[2, i, y]
            div = ux[i + 2] - ux[i] + final[1, i, y + 1] - final[1, i, y - 1]
            strain[i, y - YS] = 0.5 * (div + next_z(uz) - prev_z(uz))
        return carry

    lax.fori_loop(YS, 2 * YS, strain_row, 0)
    rows = pl.ds(pl.multiple_of(d * YS, YS), YS)

    def strain_of(t):
        x = t + HALO
        return strain.at[lax.rem(x, SL), :, x // SL]

    def send_strain(i, carry):
        t = lax.rem(d + i, ND)
        pltpu.make_async_remote_copy(
            strain_of(t), s_out.at[0, rows], st_send, st_recv,
            device_id=(g, t), device_id_type=MESH,
        ).start()
        return carry

    lax.fori_loop(1, ND, send_strain, 0)
    own_strain = pltpu.make_async_copy(strain_of(d), s_out.at[0, rows], st_self)
    own_strain.start()
    u_copies = []
    for c in range(CH):
        lo, hi = max(c * SL, HALO), min((c + 1) * SL, HALO + XS)
        if lo < hi:
            u_copies.append(
                pltpu.make_async_copy(
                    final.at[:, pl.ds(lo - c * SL, hi - lo), pl.ds(YS, YS), c],
                    u_out.at[:, pl.ds(lo - HALO, hi - lo)],
                    out_sem.at[1 + c],
                )
            )
    for c in u_copies:
        c.start()

    p_copy.wait()
    for c in u_copies:
        c.wait()
    own_strain.wait()
    part = ppad.at[pl.ds(0, (ND - 1) * YS)]
    pltpu.make_async_copy(part, part, st_send).wait()
    pltpu.make_async_copy(part, part, st_recv).wait()


def hand_over(p_in, u_in, s_in, p_out, u_out, s_out, p_buf, u_buf, s_buf, sem_in, sem_out):
    pairs = []
    half = NY // 2
    for src, buf, dst in [(p_in, p_buf, p_out), (s_in, s_buf, s_out)]:
        for j in range(2):
            part = pl.ds(j * half, half)
            pairs.append((src.at[0, part], buf.at[0, part], dst.at[0, part]))
    for c in range(3):
        for j in range(2):
            part = pl.ds(j * XS // 2, XS // 2)
            pairs.append((u_in.at[c, part], u_buf.at[c, part], u_out.at[c, part]))
    loads = [pltpu.make_async_copy(a, b, sem_in.at[i]) for i, (a, b, _) in enumerate(pairs)]
    saves = [pltpu.make_async_copy(b, c, sem_out.at[i]) for i, (_, b, c) in enumerate(pairs)]
    for c in loads:
        c.start()
    for c, s in zip(loads, saves):
        c.wait()
        s.start()
    for s in saves:
        s.wait()


def body(
    pressure_old, strain_change, storage, trans_x, trans_y, trans_z, displacement_old, modulus,
    perf_cell, perf_well, perf_count, perf_index, well_rate,
):
    dma = pltpu.SemaphoreType.DMA
    vmem = lambda *shape: pltpu.VMEM(shape, F32)
    plane = (NY, NZ)
    slabs = (SL, YW, CH, NZ)
    hbm = pl.BlockSpec(memory_space=pl.ANY)
    shapes = (
        jax.ShapeDtypeStruct((1, NY, NZ), F32),
        jax.ShapeDtypeStruct((3, XS, YS, NZ), F32),
        jax.ShapeDtypeStruct((1, NY, NZ), F32),
    )
    results = pl.pallas_call(
        kernel,
        name="poro_step",
        out_shape=shapes,
        in_specs=[hbm] * 13,
        out_specs=(hbm, hbm, hbm),
        scratch_shapes=[
            pltpu.VMEM((BLOCKS, 128), jnp.int32),
            pltpu.SMEM((BLOCKS,), jnp.int32),
            pltpu.SMEM((BLOCKS,), jnp.int32),
            vmem(BLOCKS, 128),
            vmem(1, 256),
            vmem(FLOW_SWEEPS + 1, *plane),
            vmem(*plane),
            vmem(*plane),
            vmem(*plane),
            vmem(*plane),
            vmem(*plane),
            vmem(*plane),
            vmem(*plane),
            vmem(*plane),
            vmem(*plane),
            vmem(BLOCKS, *plane),
            vmem(BLOCKS, *plane),
            vmem(2 * BLOCKS, *plane),
            vmem(FLOW_SWEEPS, *plane),
            vmem(FLOW_SWEEPS, *plane),
            pltpu.VMEM((NZ, BLOCKS * 128), jnp.bfloat16),
            vmem(2 * BLOCKS, 128),
            vmem(2 * BLOCKS, 128),
            vmem(2 * BLOCKS, 128),
            vmem(3 + FLOW_SWEEPS - 1, 8, 128),
            vmem(3 + FLOW_SWEEPS - 1, 8, 128),
            vmem(3 + FLOW_SWEEPS - 1, 8, 128),
            vmem(3, CHIPS, 128),
            vmem(FLOW_SWEEPS - 1, CHIPS, 128),
            vmem(3 * BLOCKS, CHIPS, 128),
            vmem(NY + 2 * YS, NZ),
            vmem(4, XW, YW, NZ),
            vmem(*slabs),
            vmem(3, *slabs),
            vmem(3, *slabs),
            vmem(*slabs),
            vmem(3, *slabs),
            vmem(3, *slabs),
            vmem(*slabs),
            vmem(*slabs),
            vmem(*slabs),
            vmem(*slabs),
            vmem(SL, CH, NZ),
            vmem(SL, YS, CH, NZ),
            dma((5,)),
            dma((6,)),
            dma((2,)),
            dma((2, FLOW_SWEEPS, PARTS)),
            dma((2, FLOW_SWEEPS, PARTS)),
            dma,
            dma,
            dma((2,)),
            dma((2,)),
            dma((FLOW_SWEEPS,)),
            dma((FLOW_SWEEPS,)),
            dma((FLOW_SWEEPS,)),
            dma((FLOW_SWEEPS,)),
            dma((2, 4)),
            dma((2, 4)),
            dma((2, 4)),
            dma((2, 4)),
            dma((4, CH)),
            dma((3,)),
            dma((3,)),
            dma,
            dma,
            dma,
            dma,
            dma((1 + CH,)),
        ],
        compiler_params=pltpu.CompilerParams(
            collective_id=0, has_side_effects=True, vmem_limit_bytes=62 << 20
        ),
    )(
        pressure_old, strain_change, storage, trans_x, trans_y, trans_z, displacement_old, modulus,
        perf_cell, perf_well, perf_count, perf_index,
        well_rate.reshape(1, -1),
    )
    return pl.pallas_call(
        hand_over,
        name="hand_over",
        out_shape=shapes,
        in_specs=[hbm] * 3,
        out_specs=(hbm, hbm, hbm),
        scratch_shapes=[
            vmem(1, NY, NZ),
            vmem(3, XS, YS, NZ),
            vmem(1, NY, NZ),
            dma((10,)),
            dma((10,)),
        ],
    )(*results)


def solution(mesh):
    flow = P(("grp", "dev"), None, None)
    slabs = P(None, "grp", "dev", None)
    return jax.shard_map(
        body,
        mesh=mesh,
        in_specs=(
            flow, flow, flow, flow, flow, flow, slabs, P("grp", "dev", None),
            P(("grp", "dev"), None), P(("grp", "dev")), P(("grp", "dev")), P(("grp", "dev"), None), P(),
        ),
        out_specs=(flow, slabs, flow),
        check_vma=False,
    )
```

```python
import functools

import jax
import jax.numpy as jnp
from jax import lax
from jax.experimental import pallas as pl
from jax.experimental.pallas import tpu as pltpu
from jax.sharding import PartitionSpec as P

MESH = pl.DeviceIdType.MESH
F32 = jnp.float32

FLOW_SWEEPS = 4
MECH_SWEEPS = 6
BIOT = 0.8
RELAX = 0.6
COUPLE = 0.375

NG, ND = 4, 32
NF = NG * ND
CHIPS = NF // 2
NY, NZ = 256, 256
XS, YS = 32, 8
HALO = MECH_SWEEPS + 1
CH, SL = 8, 6
XW = CH * SL
YW = 3 * YS
BLOCKS = 4
PARTS = 2
PR = NY // PARTS

ALPHA = 1.0 - RELAX * 27.0 / 26.0
BETA = RELAX / 26.0


def iota(shape, dim):
    return lax.broadcasted_iota(jnp.int32, shape, dim)


def next_z(v):
    n = v.shape[-1]
    return jnp.where(iota(v.shape, 1) == n - 1, 0.0, pltpu.roll(v, n - 1, 1))


def prev_z(v):
    return jnp.where(iota(v.shape, 1) == 0, 0.0, pltpu.roll(v, 1, 1))


def next_y(v):
    return pltpu.roll(v, v.shape[0] - 1, 0)


def prev_y(v):
    return pltpu.roll(v, 1, 0)


def extend(slots):
    return [pltpu.roll(slots[-1], 1, 0)] + slots + [pltpu.roll(slots[0], CH - 1, 0)]


def total(v):
    return jnp.sum(jnp.sum(v, axis=0, keepdims=True), axis=1, keepdims=True)


def kernel(
    p0_h, sc_h, st_h, tx_h, ty_h, tz_h, u_h, mod_h, cell_h, well_h, cnt_h, idx_h, rate_h,
    p_out, u_out, s_out,
    cell_ref, well_ref, cnt_ref, idx_ref, rate_ref,
    press, field, base, east, west, north, south, upper, lower, rdiag, wells, sinks, near,
    halo_lo, halo_hi, col_hot, near_msg, near_lo, near_hi, msg, other, joint, ag0, ag, masks,
    ppad, nat, pwin, ua, ub, gain, force, xsum, shear, dy_z, dz_z, dx_z, betas, strain,
    small_sem, load_sem, uload_sem, halo_send, halo_recv, tx_send, tx_recv, near_send, near_recv, join_send, join_recv, ag_send, ag_recv,
    usend, urecv, xsend, xrecv, relay_sem, pw_send, pw_recv, pw_self, st_send, st_recv, st_self,
    out_sem,
):
    g = lax.axis_index("grp")
    d = lax.axis_index("dev")
    f = g * ND + d
    first, last = f == 0, f == NF - 1
    has_lo, has_hi = d > 0, d < ND - 1
    has_west, has_east = g > 0, g < NG - 1

    def flow_dev(k):
        return (k // ND, lax.rem(k, ND))

    after, before = flow_dev(lax.rem(f + 1, NF)), flow_dev(lax.rem(f + NF - 1, NF))

    small_loads = [
        pltpu.make_async_copy(src, dst, small_sem.at[i])
        for i, (src, dst) in enumerate(
            [
                (cell_h, cell_ref),
                (well_h, well_ref),
                (cnt_h, cnt_ref),
                (idx_h, idx_ref),
                (rate_h, rate_ref),
            ]
        )
    ]
    plane_loads = [
        pltpu.make_async_copy(src.at[0], dst, load_sem.at[i])
        for i, (src, dst) in enumerate(
            [
                (p0_h, press.at[0]),
                (sc_h, base),
                (st_h, rdiag),
                (tx_h, east),
                (ty_h, north),
                (tz_h, upper),
            ]
        )
    ]
    own_u = pltpu.make_async_copy(
        u_h, nat.at[pl.ds(0, 3), pl.ds(HALO, XS), pl.ds(YS, YS)], uload_sem.at[0]
    )
    own_m = pltpu.make_async_copy(
        mod_h, nat.at[3, pl.ds(HALO, XS), pl.ds(YS, YS)], uload_sem.at[1]
    )
    for c in small_loads + plane_loads + [own_u, own_m]:
        c.start()

    def fill(planes, rows):
        n, m = planes.stop - planes.start, rows.stop - rows.start
        nat[0:3, planes, rows, :] = jnp.zeros((3, n, m, NZ), F32)
        nat[3, planes, rows, :] = jnp.ones((n, m, NZ), F32)

    own_planes, all_rows = slice(HALO, HALO + XS), slice(0, YW)
    fill(slice(2 * HALO + XS, XW), all_rows)
    pwin[...] = jnp.zeros(pwin.shape, F32)

    @pl.when(d == 0)
    def _():
        fill(own_planes, slice(0, YS))

    @pl.when(d == ND - 1)
    def _():
        fill(own_planes, slice(2 * YS, YW))

    @pl.when(g == 0)
    def _():
        fill(slice(0, HALO), all_rows)

    @pl.when(g == NG - 1)
    def _():
        fill(slice(HALO + XS, 2 * HALO + XS), all_rows)

    barrier = pltpu.get_barrier_semaphore()

    core, z_lo = lax.rem(g, 2), g // 2
    z_hi, phys_x, phys_y = d // 16, lax.rem(d // 4, 4), lax.rem(d, 4)
    phys_z = 2 * z_hi + z_lo
    spots = sorted(
        ((x, y) for x in range(4) for y in range(4)),
        key=lambda o: -(min(o[0], 4 - o[0]) + min(o[1], 4 - o[1])),
    )
    for ox, oy in spots:
        x, y = lax.rem(phys_x + ox, 4), lax.rem(phys_y + oy, 4)

        def greet(j, carry, x=x, y=y):
            z = lax.rem(phys_z + lax.rem(2 + 3 * (j // 2), 4), 4)
            c = lax.rem(core + 1 + lax.rem(j, 2), 2)
            pl.semaphore_signal(
                barrier, inc=1, device_id=(lax.rem(z, 2) * 2 + c, (z // 2) * 16 + x * 4 + y),
                device_id_type=MESH,
            )
            return carry

        if ox == 0 and oy == 0:
            lax.fori_loop(0, 5, greet, 0)
            lax.fori_loop(6, 8, greet, 0)
        else:
            lax.fori_loop(0, 8, greet, 0)

    @pl.when(first)
    def _():
        halo_lo[...] = jnp.zeros(halo_lo.shape, F32)
        near_lo[...] = jnp.zeros(near_lo.shape, F32)
        west[...] = jnp.zeros((NY, NZ), F32)

    @pl.when(last)
    def _():
        halo_hi[...] = jnp.zeros(halo_hi.shape, F32)
        near_hi[...] = jnp.zeros(near_hi.shape, F32)

    ppad[0:YS, :] = jnp.zeros((YS, NZ), F32)
    ppad[NY + YS :, :] = jnp.zeros((YS, NZ), F32)
    for i in range(SL):
        x = iota((CH, NZ), 0) * SL + i + g * XS - HALO
        betas[i] = jnp.where(jnp.logical_and(x >= 0, x < NG * XS), BETA, 0.0)

    for c in small_loads:
        c.wait()
    lane = iota((1, 128), 1)

    def hot(shape, index):
        return jnp.where(iota(shape, 0) == index, 1.0, 0.0).astype(jnp.bfloat16)

    def thirds(v):
        out = []
        for _ in range(3):
            part = v.astype(jnp.bfloat16)
            v = v - part.astype(F32)
            out.append(part)
        return out

    def dense(cell, value):
        at_row = iota((NY, 128), 0) == cell // NZ
        at_col = hot((NZ, 128), lax.rem(cell, NZ))
        plane = jnp.zeros((NY, NZ), F32)
        for part in thirds(value):
            spread = jnp.where(at_row, part.astype(F32), 0.0).astype(jnp.bfloat16)
            plane = plane + lax.dot_general(
                spread, at_col, (((1,), (1,)), ((), ())), preferred_element_type=F32
            )
        return plane

    weights = []
    for b in range(BLOCKS):
        weight = jnp.where(lane < cnt_ref[b], idx_ref[b : b + 1, :], 0.0)
        cell = cell_ref[b : b + 1, :]
        wells[b] = dense(cell, weight)
        col_hot[:, b * 128 : (b + 1) * 128] = hot((NZ, 128), lax.rem(cell, NZ))
        near_msg[b : b + 1, :] = cell.astype(F32)
        weights.append(weight)
    weight_sums = [jnp.sum(w, axis=1, keepdims=True) for w in weights]

    for c in plane_loads:
        c.wait()

    def start_pair(copies, to_up, to_down):
        @pl.when(to_up)
        def _():
            copies[0].start()

        @pl.when(to_down)
        def _():
            copies[1].start()

    def recv_pair(copies, to_up, to_down):
        @pl.when(to_down)
        def _():
            copies[0].wait_recv()

        @pl.when(to_up)
        def _():
            copies[1].wait_recv()

    def send_pair(copies, to_up, to_down):
        @pl.when(to_up)
        def _():
            copies[0].wait_send()

        @pl.when(to_down)
        def _():
            copies[1].wait_send()

    def halo_copies(k, j):
        part = pl.ds(j * PR, PR)
        return [
            pltpu.make_async_remote_copy(
                press.at[k, part], buffer.at[k, part], halo_send.at[s, k, j], halo_recv.at[s, k, j],
                device_id=target, device_id_type=MESH,
            )
            for s, (buffer, target) in enumerate([(halo_lo, after), (halo_hi, before)])
        ]

    tx_copy = pltpu.make_async_remote_copy(
        tx_h.at[0], west, tx_send, tx_recv, device_id=after, device_id_type=MESH
    )
    near_copies = [
        pltpu.make_async_remote_copy(
            near_msg, buffer, near_send.at[s], near_recv.at[s], device_id=target, device_id_type=MESH
        )
        for s, (buffer, target) in enumerate([(near_lo, after), (near_hi, before)])
    ]
    to_after, to_before = jnp.logical_not(last), jnp.logical_not(first)

    chip = z_lo * ND + d

    def lanes(values):
        out = jnp.zeros((1, 128), F32)
        for b, v in enumerate(values):
            out = jnp.where(lane == core * BLOCKS + b, v, out)
        return out

    def block_sums(p):
        return lanes([total(wells[b] * p) for b in range(BLOCKS)])

    def rows_of(ref, k):
        return ref.at[pl.ds(0, 3), pl.ds(0, 1)] if k == 0 else ref.at[2 + k, pl.ds(0, 1)]

    def gathered(k, r, n):
        return ag0.at[:, pl.ds(r, n)] if k == 0 else ag.at[k - 1, pl.ds(r, n)]

    def join_copy(k):
        return pltpu.make_async_remote_copy(
            rows_of(msg, k), rows_of(other, k), join_send.at[k], join_recv.at[k],
            device_id=(z_lo * 2 + 1 - core, d), device_id_type=MESH,
        )

    def start_gather(k):
        join_copy(k).wait_recv()
        for j in range(3) if k == 0 else [2 + k]:
            row = msg[j, 0:1] + other[j, 0:1]
            joint[j, 0:1] = row
            if k == 0:
                ag0[j, pl.ds(chip, 1), :] = row
            else:
                ag[k - 1, pl.ds(chip, 1), :] = row

        def send(x, y, oz):
            z = lax.rem(phys_z + oz, 4)
            pltpu.make_async_remote_copy(
                rows_of(joint, k), gathered(k, chip, 1), ag_send.at[k], ag_recv.at[k],
                device_id=(lax.rem(z, 2) * 2 + core, (z // 2) * 16 + x * 4 + y), device_id_type=MESH,
            ).start()

        for ox, oy in spots:
            x, y = lax.rem(phys_x + ox, 4), lax.rem(phys_y + oy, 4)
            if ox == 0 and oy == 0:
                for oz in (2, 1, 3):
                    send(x, y, oz)
            else:

                def step(j, carry, x=x, y=y):
                    send(x, y, lax.rem(2 + 3 * j, 4))
                    return carry

                lax.fori_loop(0, 4, step, 0)

    def gather_wait(k, sem):
        part = gathered(k, 0, CHIPS - 1)
        pltpu.make_async_copy(part, part, sem).wait()

    def y_copies(a, first_plane=0, planes=XS):
        n = HALO - 1 if a == 3 else HALO
        out = []
        for s, (k, at, to) in enumerate(
            [(lax.rem(d + 1, ND), YS - n, YS - n), (lax.rem(d + ND - 1, ND), 0, 2 * YS)]
        ):
            part = pl.ds(first_plane, planes)
            src = mod_h.at[part, pl.ds(at, n)] if a == 3 else u_h.at[a, part, pl.ds(at, n)]
            out.append(
                pltpu.make_async_remote_copy(
                    src, nat.at[a, pl.ds(HALO + first_plane, planes), pl.ds(to, n)],
                    usend.at[s, a], urecv.at[s, a], device_id=(g, k), device_id_type=MESH,
                )
            )
        return out

    def x_copies(a):
        out = []
        for s, (k, at, to) in enumerate(
            [(lax.rem(g + 1, NG), XS, 0), (lax.rem(g + NG - 1, NG), HALO, HALO + XS)]
        ):
            out.append(
                pltpu.make_async_remote_copy(
                    nat.at[a, pl.ds(at, HALO)], nat.at[a, pl.ds(to, HALO)],
                    xsend.at[s, a], xrecv.at[s, a], device_id=(k, d), device_id_type=MESH,
                )
            )
        return out

    order = [3, 0, 1, 2]
    pieces = [(a, j * XS // 2) for a in order for j in range(2)]

    def trickle(n):
        for _ in range(n):
            if pieces:
                a, at = pieces.pop(0)
                start_pair(y_copies(a, at, XS // 2), has_hi, has_lo)

    def pass_on(a):
        recv_pair(y_copies(a), has_hi, has_lo)
        start_pair(x_copies(a), has_east, has_west)

    def relay_copies(a):
        dst = gain if a == 3 else ua.at[a]
        return [
            pltpu.make_async_copy(
                nat.at[a, pl.ds(c * SL, SL)], dst.at[:, :, c], relay_sem.at[a, c]
            )
            for c in range(CH)
        ]

    def relay(a):
        recv_pair(x_copies(a), has_east, has_west)
        send_pair(x_copies(a), has_east, has_west)
        for c in relay_copies(a):
            c.start()

    pl.semaphore_wait(barrier, NF - 1)

    for j in range(PARTS):
        start_pair(halo_copies(0, j), to_after, to_before)

    @pl.when(to_after)
    def _():
        tx_copy.start()

    well_ids = [well_ref[b].astype(F32) for b in range(BLOCKS)]
    msg[0, 0:1] = block_sums(press[0])
    msg[1, 0:1] = lanes(weight_sums)
    msg[2, 0:1] = lanes([w + 1.0 for w in well_ids])
    join_copy(0).start()
    start_gather(0)

    p0 = press[0]
    storage = rdiag[...]
    base[...] = storage * p0 - BIOT * base[...]
    east[...] = jnp.where(last, 0.0, east[...])
    north[...] = jnp.where(iota((NY, NZ), 0) == NY - 1, 0.0, north[...])
    south[...] = prev_y(north[...])
    upper[...] = jnp.where(iota((NY, NZ), 1) == NZ - 1, 0.0, upper[...])
    lower[...] = pltpu.roll(upper[...], 1, 1)
    partial_sum = storage + east[...] + north[...] + south[...] + upper[...] + lower[...]
    for b in range(BLOCKS):
        partial_sum = partial_sum + wells[b]
    rdiag[...] = partial_sum
    own_u.wait()
    own_m.wait()

    def own_terms(p):
        acc = base[...] + north[...] * next_y(p) + south[...] * prev_y(p)
        return acc + upper[...] * pltpu.roll(p, NZ - 1, 1) + lower[...] * pltpu.roll(p, 1, 1)

    rates, strengths = [], []

    def find_wells():
        rate_at = iota((1, 256), 1).astype(F32)
        for n, (at_g, at_d) in enumerate([(g, d), before, after]):
            row = (at_g // 2) * ND + at_d
            first_lane = lax.rem(at_g, 2) * BLOCKS
            ids = ag0[2, pl.ds(row, 1), :]
            for b in range(BLOCKS):
                well = jnp.sum(jnp.where(lane == first_lane + b, ids, 0.0), axis=1, keepdims=True)
                mask = jnp.where(ag0[2] == well, 1.0, 0.0)
                masks[n * BLOCKS + b] = mask
                strengths.append(total(mask * ag0[1]))
                rates.append(
                    jnp.sum(
                        jnp.where(rate_at == well - 1.0, rate_ref[...], 0.0), axis=1, keepdims=True
                    )
                )

    def bottoms_of(k, count):
        sums = ag0[0] if k == 0 else ag[k - 1]
        return [(rates[n] + total(masks[n] * sums)) / strengths[n] for n in range(count)]

    for k in range(FLOW_SWEEPS + 1):
        if k == 0:
            field[...] = own_terms(p0)

            @pl.when(to_before)
            def _():
                tx_copy.wait_recv()

            rdiag[...] = 1.0 / (rdiag[...] + west[...])
            gather_wait(0, ag_recv.at[0])
            find_wells()
            bottoms = bottoms_of(0, BLOCKS)
            inflow = wells[0] * bottoms[0]
            for b in range(1, BLOCKS):
                inflow = inflow + wells[b] * bottoms[b]
            field[...] += inflow
        elif k == 1:
            p = press[1]
        else:
            gather_wait(k - 1, ag_recv.at[k - 1])
            bottoms = bottoms_of(k - 1, 3 * BLOCKS if k < FLOW_SWEEPS else BLOCKS)
            p = press[k]
            for b in range(BLOCKS):
                p = p + sinks[b] * bottoms[b]
        if k == FLOW_SWEEPS:
            ppad[YS : YS + NY, :] = p
            break
        if k > 0:
            msg[2 + k, 0:1] = block_sums(p)
            join_copy(k).start()
            field[...] = own_terms(p)
            start_gather(k)
        if k > 1:
            from_lo = near[0] * bottoms[BLOCKS]
            from_hi = near[BLOCKS] * bottoms[2 * BLOCKS]
            for b in range(1, BLOCKS):
                from_lo = from_lo + near[b] * bottoms[BLOCKS + b]
                from_hi = from_hi + near[BLOCKS + b] * bottoms[2 * BLOCKS + b]
            field[...] += east[...] * from_hi + west[...] * from_lo
        for j in range(PARTS):
            send_pair(halo_copies(k, j), to_after, to_before)
        trickle([0, 2, 2, 2][k])
        for j in range(PARTS):
            part = slice(j * PR, (j + 1) * PR)
            recv_pair(halo_copies(k, j), to_after, to_before)
            acc = field[part] + east[part] * halo_hi[k, part] + west[part] * halo_lo[k, part]
            press[k + 1, part] = acc * rdiag[part]
            if k < FLOW_SWEEPS - 1:
                start_pair(halo_copies(k + 1, j), to_after, to_before)
        if k == 0:
            found = jnp.zeros((NY, BLOCKS * 128), F32)
            for third in thirds(rdiag[...]):
                found = found + jnp.dot(third, col_hot[...], preferred_element_type=F32)
            for b in range(BLOCKS):
                at_row = iota((NY, 128), 0) == cell_ref[b : b + 1, :] // NZ
                at_cell = jnp.where(at_row, found[:, b * 128 : (b + 1) * 128], 0.0)
                at_cell = jnp.sum(at_cell, axis=0, keepdims=True)
                near_msg[BLOCKS + b : BLOCKS + b + 1, :] = weights[b] * at_cell
                sinks[b] = wells[b] * rdiag[...]
            start_pair(near_copies, to_after, to_before)
        if k == 1:
            recv_pair(near_copies, to_after, to_before)
            for s, buffer in enumerate([near_lo, near_hi]):
                for b in range(BLOCKS):
                    near[s * BLOCKS + b] = dense(
                        buffer[b : b + 1, :].astype(jnp.int32), buffer[BLOCKS + b : BLOCKS + b + 1, :]
                    )

    def window(t):
        return ppad.at[pl.ds(pl.multiple_of(t * YS, YS), YW)]

    def place(x):
        return pwin.at[lax.rem(x, SL), :, x // SL]

    own_window = pltpu.make_async_copy(window(d), place(HALO + d), pw_self)
    own_window.start()

    def spread(first_step, x, target, j):
        def send(i, carry):
            t = lax.rem(d + i, ND)
            pltpu.make_async_remote_copy(
                window(t), place(x), pw_send.at[j], pw_recv.at[j],
                device_id=(target, t), device_id_type=MESH,
            ).start()
            return carry

        lax.fori_loop(first_step, ND, send, 0)

    spread(1, HALO + d, g, 0)
    to_hi = jnp.logical_and(d >= XS - HALO, has_east)
    to_lo = jnp.logical_and(d < HALO, has_west)

    @pl.when(to_hi)
    def _():
        spread(0, d - (XS - HALO), g + 1, 1)

    @pl.when(to_lo)
    def _():
        spread(0, HALO + XS + d, g - 1, 2)

    p_copy = pltpu.make_async_copy(ppad.at[pl.ds(YS, NY)], p_out.at[0], out_sem.at[0])
    p_copy.start()
    trickle(16)

    def window_wait(count, sem):
        part = nat.at[0, pl.ds(0, count)]
        pltpu.make_async_copy(part, part, sem).wait()

    pass_on(order[0])
    pass_on(order[1])
    pass_on(order[2])
    relay(order[0])
    relay(order[1])
    for c in relay_copies(3):
        c.wait()

    def gain_row(y, carry):
        gy = (d - 1) * YS + y
        inside = jnp.logical_and(gy >= 0, gy < NY)
        scale = jnp.where(inside, -0.5 * BIOT / BETA * RELAX / 26.0, 0.0)
        for i in range(SL):
            gain[i, y] = scale * betas[i] / gain[i, y]
        return carry

    lax.fori_loop(2, YW - 2, gain_row, 0)
    pass_on(order[3])
    relay(order[2])
    relay(order[3])
    for a in range(3):
        for c in relay_copies(a):
            c.wait()

    @pl.when(jnp.logical_not(last))
    def _():
        tx_copy.wait_send()

    for k in range(FLOW_SWEEPS):
        gather_wait(k, ag_send.at[k])
        join_copy(k).wait_send()
    send_pair(near_copies, to_after, to_before)
    for a in range(4):
        send_pair(y_copies(a), has_hi, has_lo)
    window_wait(ND - 1, pw_send.at[0])

    @pl.when(to_hi)
    def _():
        window_wait(ND, pw_send.at[1])

    @pl.when(to_lo)
    def _():
        window_wait(ND, pw_send.at[2])

    own_window.wait()
    window_wait(ND - 1, pw_recv.at[0])

    @pl.when(has_west)
    def _():
        window_wait(HALO, pw_recv.at[1])

    @pl.when(has_east)
    def _():
        window_wait(HALO, pw_recv.at[2])

    def force_row(y, carry):
        p = extend([pwin[i, y] for i in range(SL)])
        for i in range(SL):
            r = gain[i, y]
            force[0, i, y] = r * (p[i + 2] - p[i])
            force[1, i, y] = r * (pwin[i, y + 1] - pwin[i, y - 1])
            force[2, i, y] = r * (next_z(p[i + 1]) - prev_z(p[i + 1]))
        return carry

    lax.fori_loop(2, YW - 2, force_row, 0)

    def sweep_tools(s):
        src, dst = (ua, ub) if s % 2 == 0 else (ub, ua)

        def row_values(y, src=src):
            tz, dz = [], []
            for c in range(3):
                t, q = [], []
                for i in range(SL):
                    v = src[c, i, y]
                    hi, lo = next_z(v), prev_z(v)
                    t.append(v + hi + lo)
                    q.append(hi - lo)
                tz.append(extend(t))
                dz.append(q)
            sums = []
            for t in tz:
                r = []
                for i in range(0, SL, 2):
                    pair = t[i + 1] + t[i + 2]
                    r += [t[i] + pair, pair + t[i + 3]]
                sums.append(r)
            ux = extend([src[0, i, y] for i in range(SL)])
            dx = extend(dz[0])
            along_y = [ux[i + 2] - ux[i] + dz[2][i] for i in range(SL)]
            cross = [dx[i + 2] - dx[i] for i in range(SL)]
            return sums, along_y, dz[1], dz[2], cross

        def row_store(y, values):
            sums, along_y, dzy, dzz, cross = values
            for i in range(SL):
                for c in range(3):
                    xsum[c, i, y] = sums[c][i]
                shear[i, y] = along_y[i]
                dy_z[i, y] = dzy[i]
                dz_z[i, y] = dzz[i]
                dx_z[i, y] = cross[i]

        def combine(y, src=src, dst=dst):
            gy = (d - 1) * YS + y
            inside = jnp.logical_and(gy >= 0, gy < NY).astype(F32)
            along_x = extend([src[1, i, y + 1] - src[1, i, y - 1] + dz_z[i, y] for i in range(SL)])
            for i in range(SL):
                beta = betas[i] * inside
                mixed = [
                    along_x[i + 2] - along_x[i],
                    shear[i, y + 1] - shear[i, y - 1],
                    dx_z[i, y] + dy_z[i, y + 1] - dy_z[i, y - 1],
                ]
                for c in range(3):
                    box = xsum[c, i, y - 1] + xsum[c, i, y] + xsum[c, i, y + 1]
                    r = box + COUPLE * mixed[c] + (ALPHA / BETA) * src[c, i, y]
                    dst[c, i, y] = beta * r + force[c, i, y]

        return row_values, row_store, combine

    def first_rows(s, row_values):
        return [(y, row_values(y)) for y in (1 + s, 2 + s, 3 + s)]

    tools = [sweep_tools(s) for s in range(MECH_SWEEPS)]
    for y, values in first_rows(0, tools[0][0]):
        tools[0][1](y, values)
    for s, (row_values, row_store, combine) in enumerate(tools):
        y0, y1 = 2 + s, YW - 2 - s

        def mech_row(y, carry, row_values=row_values, row_store=row_store, combine=combine):
            values = row_values(y + 2)
            combine(y)
            row_store(y + 2, values)
            return carry

        lax.fori_loop(y0, y1 - 2, mech_row, 0, unroll=2)
        values = row_values(y1)
        combine(y1 - 2)
        row_store(y1, values)
        ahead = first_rows(s + 1, tools[s + 1][0]) if s < MECH_SWEEPS - 1 else []
        combine(y1 - 1)
        for y, values in ahead:
            row_store(y, values)

    final = ua if MECH_SWEEPS % 2 == 0 else ub

    def strain_row(y, carry):
        ux = extend([final[0, i, y] for i in range(SL)])
        for i in range(SL):
            uz = final[2, i, y]
            div = ux[i + 2] - ux[i] + final[1, i, y + 1] - final[1, i, y - 1]
            strain[i, y - YS] = 0.5 * (div + next_z(uz) - prev_z(uz))
        return carry

    lax.fori_loop(YS, 2 * YS, strain_row, 0)
    rows = pl.ds(pl.multiple_of(d * YS, YS), YS)

    def strain_of(t):
        x = t + HALO
        return strain.at[lax.rem(x, SL), :, x // SL]

    def send_strain(i, carry):
        t = lax.rem(d + i, ND)
        pltpu.make_async_remote_copy(
            strain_of(t), s_out.at[0, rows], st_send, st_recv,
            device_id=(g, t), device_id_type=MESH,
        ).start()
        return carry

    lax.fori_loop(1, ND, send_strain, 0)
    own_strain = pltpu.make_async_copy(strain_of(d), s_out.at[0, rows], st_self)
    own_strain.start()
    u_copies = []
    for c in range(CH):
        lo, hi = max(c * SL, HALO), min((c + 1) * SL, HALO + XS)
        if lo < hi:
            u_copies.append(
                pltpu.make_async_copy(
                    final.at[:, pl.ds(lo - c * SL, hi - lo), pl.ds(YS, YS), c],
                    u_out.at[:, pl.ds(lo - HALO, hi - lo)],
                    out_sem.at[1 + c],
                )
            )
    for c in u_copies:
        c.start()

    p_copy.wait()
    for c in u_copies:
        c.wait()
    own_strain.wait()
    part = ppad.at[pl.ds(0, (ND - 1) * YS)]
    pltpu.make_async_copy(part, part, st_send).wait()
    pltpu.make_async_copy(part, part, st_recv).wait()


def hand_over(p_in, u_in, s_in, p_out, u_out, s_out, p_buf, u_buf, s_buf, sem_in, sem_out):
    pairs = []
    half = NY // 2
    for src, buf, dst in [(p_in, p_buf, p_out), (s_in, s_buf, s_out)]:
        for j in range(2):
            part = pl.ds(j * half, half)
            pairs.append((src.at[0, part], buf.at[0, part], dst.at[0, part]))
    for c in range(3):
        for j in range(2):
            part = pl.ds(j * XS // 2, XS // 2)
            pairs.append((u_in.at[c, part], u_buf.at[c, part], u_out.at[c, part]))
    loads = [pltpu.make_async_copy(a, b, sem_in.at[i]) for i, (a, b, _) in enumerate(pairs)]
    saves = [pltpu.make_async_copy(b, c, sem_out.at[i]) for i, (_, b, c) in enumerate(pairs)]
    for c in loads:
        c.start()
    for c, s in zip(loads, saves):
        c.wait()
        s.start()
    for s in saves:
        s.wait()


def body(
    pressure_old, strain_change, storage, trans_x, trans_y, trans_z, displacement_old, modulus,
    perf_cell, perf_well, perf_count, perf_index, well_rate,
):
    dma = pltpu.SemaphoreType.DMA
    vmem = lambda *shape: pltpu.VMEM(shape, F32)
    plane = (NY, NZ)
    slabs = (SL, YW, CH, NZ)
    hbm = pl.BlockSpec(memory_space=pl.ANY)
    shapes = (
        jax.ShapeDtypeStruct((1, NY, NZ), F32),
        jax.ShapeDtypeStruct((3, XS, YS, NZ), F32),
        jax.ShapeDtypeStruct((1, NY, NZ), F32),
    )
    results = pl.pallas_call(
        kernel,
        name="poro_step",
        out_shape=shapes,
        in_specs=[hbm] * 13,
        out_specs=(hbm, hbm, hbm),
        scratch_shapes=[
            pltpu.VMEM((BLOCKS, 128), jnp.int32),
            pltpu.SMEM((BLOCKS,), jnp.int32),
            pltpu.SMEM((BLOCKS,), jnp.int32),
            vmem(BLOCKS, 128),
            vmem(1, 256),
            vmem(FLOW_SWEEPS + 1, *plane),
            vmem(*plane),
            vmem(*plane),
            vmem(*plane),
            vmem(*plane),
            vmem(*plane),
            vmem(*plane),
            vmem(*plane),
            vmem(*plane),
            vmem(*plane),
            vmem(BLOCKS, *plane),
            vmem(BLOCKS, *plane),
            vmem(2 * BLOCKS, *plane),
            vmem(FLOW_SWEEPS, *plane),
            vmem(FLOW_SWEEPS, *plane),
            pltpu.VMEM((NZ, BLOCKS * 128), jnp.bfloat16),
            vmem(2 * BLOCKS, 128),
            vmem(2 * BLOCKS, 128),
            vmem(2 * BLOCKS, 128),
            vmem(3 + FLOW_SWEEPS - 1, 8, 128),
            vmem(3 + FLOW_SWEEPS - 1, 8, 128),
            vmem(3 + FLOW_SWEEPS - 1, 8, 128),
            vmem(3, CHIPS, 128),
            vmem(FLOW_SWEEPS - 1, CHIPS, 128),
            vmem(3 * BLOCKS, CHIPS, 128),
            vmem(NY + 2 * YS, NZ),
            vmem(4, XW, YW, NZ),
            vmem(*slabs),
            vmem(3, *slabs),
            vmem(3, *slabs),
            vmem(*slabs),
            vmem(3, *slabs),
            vmem(3, *slabs),
            vmem(*slabs),
            vmem(*slabs),
            vmem(*slabs),
            vmem(*slabs),
            vmem(SL, CH, NZ),
            vmem(SL, YS, CH, NZ),
            dma((5,)),
            dma((6,)),
            dma((2,)),
            dma((2, FLOW_SWEEPS, PARTS)),
            dma((2, FLOW_SWEEPS, PARTS)),
            dma,
            dma,
            dma((2,)),
            dma((2,)),
            dma((FLOW_SWEEPS,)),
            dma((FLOW_SWEEPS,)),
            dma((FLOW_SWEEPS,)),
            dma((FLOW_SWEEPS,)),
            dma((2, 4)),
            dma((2, 4)),
            dma((2, 4)),
            dma((2, 4)),
            dma((4, CH)),
            dma((3,)),
            dma((3,)),
            dma,
            dma,
            dma,
            dma,
            dma((1 + CH,)),
        ],
        compiler_params=pltpu.CompilerParams(
            collective_id=0, has_side_effects=True, vmem_limit_bytes=62 << 20
        ),
    )(
        pressure_old, strain_change, storage, trans_x, trans_y, trans_z, displacement_old, modulus,
        perf_cell, perf_well, perf_count, perf_index,
        well_rate.reshape(1, -1),
    )
    return pl.pallas_call(
        hand_over,
        name="hand_over",
        out_shape=shapes,
        in_specs=[hbm] * 3,
        out_specs=(hbm, hbm, hbm),
        scratch_shapes=[
            vmem(1, NY, NZ),
            vmem(3, XS, YS, NZ),
            vmem(1, NY, NZ),
            dma((10,)),
            dma((10,)),
        ],
    )(*results)


def solution(mesh):
    flow = P(("grp", "dev"), None, None)
    slabs = P(None, "grp", "dev", None)
    return jax.shard_map(
        body,
        mesh=mesh,
        in_specs=(
            flow, flow, flow, flow, flow, flow, slabs, P("grp", "dev", None),
            P(("grp", "dev"), None), P(("grp", "dev")), P(("grp", "dev")), P(("grp", "dev"), None), P(),
        ),
        out_specs=(flow, slabs, flow),
        check_vma=False,
    )
```
